32 devices in a mesh: req: 8 (over y, x, core), tp: 4 (over z).
Axes of the slice: x: 2, y: 2, z: 4, core: 2. Of those that a mesh axis runs over, the one named last changes fastest.
Arguments:
- hidden: bfloat16 [8, 8192], P(None, 'req')
- attn_gain: bfloat16 [2, 8192], P(None, 'req'), may hold values from 0.5 to 1.5
- q_weight: bfloat16 [2, 8192, 4096], P(None, 'req', 'tp'), may hold values from -0.0625 to 0.0625
- o_weight: bfloat16 [2, 4096, 8192], P(None, 'tp', 'req'), may hold values from -0.09375 to 0.09375
- ffn_gain: bfloat16 [2, 8192], P(None, 'req'), may hold values from 0.5 to 1.5
- gate_weight: bfloat16 [2, 8192, 14336], P(None, 'req', 'tp'), may hold values from -0.0625 to 0.0625
- up_weight: bfloat16 [2, 8192, 14336], P(None, 'req', 'tp'), may hold values from -0.0625 to 0.0625
- down_weight: bfloat16 [2, 14336, 8192], P(None, 'tp', 'req'), may hold values from -0.046875 to 0.046875
- kv_pool: bfloat16 [2, 256, 4, 2, 128, 128], P(None, 'req', 'tp')
- block_home: int32 [8, 32], P('req'), may hold values from 0 to 255, as said below
- chosen: int32 [2, 8, 4, 24], P(None, 'req', 'tp'), may hold values from 0 to 31, as said below
- chosen_count: int32 [2, 8, 4], P(None, 'req', 'tp'), may hold values from 6 to 24
Outputs:
- new_hidden: bfloat16 [8, 8192], P(None, 'req')
The draws below stay inside these ranges and needn't reach their ends.
Inputs may be any that keep to these rules, and one draw needn't show every extreme that they name: `block_home`: pool slot p lies on store device p // 32 of req; every slot belongs to exactly one block of one request, and every request has exactly 4 blocks on each store device. `chosen`: entries of a list are distinct. The used entries of a list are all 4 blocks of some store devices and some blocks of one more; entries from chosen_count on are ignored.
All inputs are finite; a program needn't handle non-finite values.
Results may differ from the reference program's by a relative error of at most 0.038.
Values may be sent and summed in bfloat16 or wider, within the bound.
A program may use at most 128 MiB of HBM per device.

```python
import math
import jax
import jax.numpy as jnp
from jax import lax

D = 8192
FF = 14336
HK = 4
QPK = 8
HD = 128
BLOCK = 128
CTX_BLK = 32
MAXSEL = 24
LAYERS = 2
REQ_DEV = 1
REQUESTS = 8
POOL = 256
PER_STORE = 4
SEL_MIN = 6


def store_layout(key):
    order_scores = jax.random.randint(key, (REQUESTS, CTX_BLK), 0, 1 << 20) * CTX_BLK + jnp.arange(CTX_BLK)[None, :]
    return jnp.argsort(order_scores, axis=1).astype(jnp.int32)


def draw_block_home(key, part):
    order = store_layout(key)
    key = jax.random.fold_in(key, 5)
    stores_n = CTX_BLK // PER_STORE
    pool_dev = REQ_DEV * CTX_BLK
    position = jnp.argsort(order, axis=1).astype(jnp.int32)
    store_of = position % stores_n
    within = position // stores_n
    slot_scores = jax.random.randint(key, (stores_n, pool_dev), 0, 1 << 20) * pool_dev + jnp.arange(pool_dev)[None, :]
    slot_perm = jnp.argsort(slot_scores, axis=1).astype(jnp.int32)
    request = jnp.arange(REQUESTS)[:, None]
    slot_of = slot_perm[store_of, request * PER_STORE + within]
    return (store_of * pool_dev + slot_of).astype(jnp.int32)


def draw_chosen(key, part):
    order = store_layout(key)
    key = jax.random.fold_in(key, 7)
    stores_n = CTX_BLK // PER_STORE
    store_scores = jax.random.randint(key, (LAYERS, REQUESTS, HK, stores_n), 0, 1 << 20) * stores_n + jnp.arange(stores_n)
    store_order = jnp.argsort(store_scores, axis=3).astype(jnp.int32)
    entry = jnp.arange(MAXSEL)
    picked_store = store_order[..., entry // PER_STORE]
    position = picked_store + entry % PER_STORE * stores_n
    request = jnp.arange(REQUESTS)[None, :, None, None]
    return order[request, position].astype(jnp.int32)


def draw_chosen_count(key, part):
    key = jax.random.fold_in(key, 9)
    count_key, spot_key = jax.random.split(key)
    counts = jax.random.randint(count_key, (LAYERS, REQUESTS, HK), SEL_MIN, MAXSEL + 1)
    flat_counts = counts.reshape(-1)
    spot = jax.random.randint(spot_key, (), 0, flat_counts.shape[0])
    flat_counts = flat_counts.at[spot].set(MAXSEL)
    return flat_counts.reshape(LAYERS, REQUESTS, HK).astype(jnp.int32)


def draw_kv_pool(key, part):
    key = jax.random.fold_in(key, 11)
    shape_all = (LAYERS, POOL, HK, 2, BLOCK, HD)
    normal_key = jax.random.fold_in(key, 0)
    which_part = jnp.arange(2).reshape(1, 1, 1, 2, 1, 1)
    base = jnp.clip(jax.random.normal(normal_key, shape_all, jnp.float32), -6.0, 6.0)
    return (base * jnp.where(which_part == 0, 1.9, 1.0)).astype(jnp.bfloat16)


def draw_hidden(key, part):
    key = jax.random.fold_in(key, 13)
    normal_key = jax.random.fold_in(key, 0)
    column_ramp = 0.3 * jnp.exp(jnp.arange(D).astype(jnp.float32) * (math.log(3.0) / D))
    base = jnp.clip(jax.random.normal(normal_key, (REQUESTS, D), jnp.float32), -6.0, 6.0)
    return (base * column_ramp[None, :]).astype(jnp.bfloat16)


def steps_of(stream_key, extent, cuts, low, largest):
    def one(dim, shards_of):
        steps = jax.random.uniform(jax.random.fold_in(jax.random.fold_in(stream_key, 6), dim), (shards_of,), jnp.float32, low / len(cuts), largest / len(cuts))
        return jnp.repeat(jnp.exp(steps), extent[dim] // shards_of).reshape((-1,) + (1,) * (len(extent) - dim - 1))

    level = one(*cuts[0])
    for cut in cuts[1:]:
        level = level * one(*cut)
    return level


def centred(rng, dims, deviation, most, cuts=(), kind=jnp.bfloat16):
    result = jax.random.normal(rng, dims, jnp.float32) * deviation
    if len(cuts) > 0:
        result = steps_of(rng, dims, cuts, -0.22, 0.18) * result
    return jnp.clip(result, min=-most, max=most).astype(kind)


def setup_inputs(seed: int = 0) -> dict:
    key_list = jax.random.split(jax.random.key(seed), 13)
    hidden = draw_hidden(jax.random.fold_in(key_list[12], 71), 0)
    attn_gain = jnp.clip(1.0 + 0.1 * jax.random.normal(key_list[1], (LAYERS, D), jnp.float32), 0.5, 1.5).astype(jnp.bfloat16)
    q_weight = centred(key_list[2], (LAYERS, D, HK * QPK * HD), D ** -0.5, 0.0625, ((1, 8), (2, 4)))
    o_weight = centred(key_list[3], (LAYERS, HK * QPK * HD, D), (HK * QPK * HD) ** -0.5, 0.09375, ((1, 4), (2, 8)))
    ffn_gain = jnp.clip(1.0 + 0.1 * jax.random.normal(key_list[4], (LAYERS, D), jnp.float32), 0.5, 1.5).astype(jnp.bfloat16)
    gate_weight = centred(key_list[5], (LAYERS, D, FF), D ** -0.5, 0.0625, ((1, 8), (2, 4)))
    up_weight = centred(key_list[6], (LAYERS, D, FF), D ** -0.5, 0.0625, ((1, 8), (2, 4)))
    down_weight = centred(key_list[7], (LAYERS, FF, D), FF ** -0.5, 0.046875, ((1, 4), (2, 8)))
    kv_pool = draw_kv_pool(jax.random.fold_in(key_list[12], 71), 0)
    block_home = draw_block_home(jax.random.fold_in(key_list[12], 71), 0)
    chosen = draw_chosen(jax.random.fold_in(key_list[12], 71), 0)
    chosen_count = draw_chosen_count(jax.random.fold_in(key_list[12], 71), 0)
    return {"hidden": hidden, "attn_gain": attn_gain, "q_weight": q_weight, "o_weight": o_weight, "ffn_gain": ffn_gain, "gate_weight": gate_weight, "up_weight": up_weight, "down_weight": down_weight, "kv_pool": kv_pool, "block_home": block_home, "chosen": chosen, "chosen_count": chosen_count}


MASK_FILL = -1e+30
EPSILON = 1e-05

def rotary(queries, position):
    head_size = queries.shape[-1]
    half_size = head_size // 2
    freq_idx = jnp.arange(half_size).astype(queries.dtype)
    angles = position * jnp.exp(freq_idx * (-2.0 * math.log(500000.0) / head_size))
    cosine = jnp.cos(angles)
    sine_part = jnp.sin(angles)
    lower_half = queries[..., :half_size]
    upper_half = queries[..., half_size:]
    return jnp.concatenate([lower_half * cosine - upper_half * sine_part, upper_half * cosine + lower_half * sine_part], axis=-1)

def inverse_rms(current):
    widened = current.astype(jnp.float32)
    return lax.rsqrt(lax.optimization_barrier(jnp.mean(widened * widened, axis=1)) + EPSILON)

def apply_gain(current, gain):
    return (current.astype(jnp.float32) * gain.astype(jnp.float32)).astype(jnp.bfloat16)

def attend_request(query_r, pool_ids, count_r, pool_layer):
    head_index = jnp.arange(pool_ids.shape[0])[:, None]
    blocks = pool_layer[pool_ids, head_index]
    key_part = blocks[:, :, 0].astype(jnp.float32)
    value_part = blocks[:, :, 1].astype(jnp.float32)
    scores = jnp.einsum('geh,gkbh->gekb', query_r.astype(jnp.float32), key_part, precision=lax.Precision.HIGHEST)
    block_max = lax.optimization_barrier(jnp.max(scores, axis=3))
    exp_terms = jnp.exp(scores - block_max[..., None])
    block_sum = lax.optimization_barrier(jnp.sum(exp_terms, axis=3))
    weights = lax.optimization_barrier(exp_terms.astype(jnp.bfloat16)).astype(jnp.float32)
    block_acc = jnp.einsum('gekb,gkbh->gekh', weights, value_part, precision=lax.Precision.HIGHEST)
    used_mask = jnp.arange(pool_ids.shape[1])[None, :] < count_r[:, None]
    block_max = jnp.where(used_mask[:, None, :], block_max, MASK_FILL)
    overall = lax.optimization_barrier(jnp.max(block_max, axis=2, keepdims=True))
    rescale = jnp.exp(block_max - overall)
    numerator = lax.optimization_barrier(jnp.sum(rescale[..., None] * block_acc, axis=2))
    denominator = lax.optimization_barrier(jnp.sum(rescale * block_sum, axis=2))
    return (numerator / denominator[..., None]).astype(jnp.bfloat16)

def reference(hidden, attn_gain, q_weight, o_weight, ffn_gain, gate_weight, up_weight, down_weight, kv_pool, block_home, chosen, chosen_count):
    position = float(CTX_BLK * BLOCK - 1)
    current = hidden
    row_index = jnp.arange(current.shape[0])[:, None, None]
    for layer_no in range(LAYERS):
        inv = inverse_rms(current)
        scaled = apply_gain(current, attn_gain[layer_no])
        queries = jnp.dot(scaled, q_weight[layer_no], preferred_element_type=jnp.float32) * inv[:, None]
        queries = queries.reshape(current.shape[0], HK, QPK, HD)
        queries = (rotary(queries, position) * HD ** (-0.5)).astype(jnp.bfloat16)
        pool_ids = block_home[row_index, chosen[layer_no]].astype(jnp.int32)
        pool_layer = kv_pool[layer_no]
        context = lax.map(lambda packed: attend_request(packed[0], packed[1], packed[2], pool_layer), (queries, pool_ids, chosen_count[layer_no]))
        context = context.reshape(current.shape[0], HK * QPK * HD)
        attended = (current.astype(jnp.float32) + jnp.dot(context, o_weight[layer_no], preferred_element_type=jnp.float32)).astype(jnp.bfloat16)
        inv2 = inverse_rms(attended)
        scaled = apply_gain(attended, ffn_gain[layer_no])
        gate = jnp.dot(scaled, gate_weight[layer_no], preferred_element_type=jnp.float32) * inv2[:, None]
        up_part = jnp.dot(scaled, up_weight[layer_no], preferred_element_type=jnp.float32) * inv2[:, None]
        activated = (jax.nn.silu(gate) * up_part).astype(jnp.bfloat16)
        current = (attended.astype(jnp.float32) + jnp.dot(activated, down_weight[layer_no], preferred_element_type=jnp.float32)).astype(jnp.bfloat16)
    return current
```

```python
import functools
import math

import jax
import jax.numpy as jnp
import numpy as np
from jax import lax
from jax.experimental import pallas as pl
from jax.experimental.pallas import tpu as pltpu
from jax.sharding import PartitionSpec as P

D = 8192
LAYERS = 2


MASK_FILL = -1e30
EPSILON = 1e-05
MESH = pl.DeviceIdType.MESH
LANES = 128
TOKENS = 512
WIDE = 512
MIB = 1 << 20


def rotary(queries, position):
    head_size = queries.shape[-1]
    half_size = head_size // 2
    freq_idx = jnp.arange(half_size).astype(queries.dtype)
    angles = position * jnp.exp(freq_idx * (-2.0 * math.log(500000.0) / head_size))
    cosine = jnp.cos(angles)
    sine_part = jnp.sin(angles)
    lower_half = queries[..., :half_size]
    upper_half = queries[..., half_size:]
    return jnp.concatenate(
        [
            lower_half * cosine - upper_half * sine_part,
            upper_half * cosine + lower_half * sine_part,
        ],
        axis=-1,
    )


def local_squares(current):
    widened = current.astype(jnp.float32)
    return jnp.sum(widened * widened, axis=1)


def apply_gain(current, gain):
    return (current.astype(jnp.float32) * gain.astype(jnp.float32)).astype(jnp.bfloat16)


def inverse_of(squares):
    return lax.rsqrt(squares / D + EPSILON)


def summed_inverse(current):
    return inverse_of(lax.psum(local_squares(current), "req"))


def sum_over_heads(partial_sum):
    return lax.psum(partial_sum, "tp")


def block_stats(queries, blocks, valid):
    scores = jnp.einsum(
        "sigeh,sigqbh->sigeqb", queries, blocks[:, :, :, :, 0], preferred_element_type=jnp.float32
    )
    block_max = jnp.max(scores, axis=5)
    exp_terms = jnp.exp(scores - block_max[..., None])
    block_sum = jnp.sum(exp_terms, axis=5)
    block_acc = jnp.einsum(
        "sigeqb,sigqbh->sigeqh",
        exp_terms.astype(jnp.bfloat16),
        blocks[:, :, :, :, 1],
        preferred_element_type=jnp.float32,
    )
    block_max = jnp.where(valid[:, :, :, None, :], block_max, MASK_FILL)
    return (block_max, block_sum, block_acc)


def combine(block_max, block_sum, block_acc, axes):
    overall = jnp.max(block_max, axis=axes, keepdims=True)
    rescale = jnp.exp(block_max - overall)
    numerator = jnp.sum(rescale[..., None] * block_acc, axis=axes)
    denominator = jnp.sum(rescale * block_sum, axis=axes)
    return (jnp.squeeze(overall, axes), denominator, numerator)


def shards(
    hidden,
    attn_gain,
    q_weight,
    o_weight,
    ffn_gain,
    gate_weight,
    up_weight,
    down_weight,
    kv_pool,
    block_home,
    chosen,
    chosen_count,
):
    n_req = lax.axis_size("req")
    req_dev = chosen.shape[1]
    heads_dev = chosen.shape[2]
    most_sel = chosen.shape[3]
    pool_dev = kv_pool.shape[1]
    head_size = kv_pool.shape[5]
    per_store = block_home.shape[1] // n_req
    position = float(block_home.shape[1] * kv_pool.shape[4] - 1)
    own_start = lax.axis_index("req") * req_dev
    row_index = jnp.arange(req_dev)[:, None, None]
    entries = jnp.arange(most_sel)
    store_ids = jnp.arange(n_req)[:, None, None, None, None]
    slot_ids = jnp.arange(per_store)[None, None, None, :, None]
    head_index = jnp.arange(heads_dev)[None, None, :, None]
    current = hidden
    for layer_no in range(LAYERS):
        scaled = apply_gain(current, attn_gain[layer_no])
        inv_all = summed_inverse(current)
        rows_in = scaled
        product = jnp.dot(rows_in, q_weight[layer_no], preferred_element_type=jnp.float32)
        summed = lax.psum_scatter(product, "req", scatter_dimension=0, tiled=True)
        inv_own = lax.dynamic_slice_in_dim(inv_all, own_start, req_dev, 0)
        queries = (summed * inv_own[:, None]).reshape(req_dev, heads_dev, -1, head_size)
        queries = (rotary(queries, position) * head_size ** (-0.5)).astype(jnp.bfloat16)
        pool_ids = block_home[row_index, chosen[layer_no]]
        home_store = pool_ids // pool_dev
        home_slot = pool_ids % pool_dev
        used_mask = entries[None, None, :] < chosen_count[layer_no][:, :, None]
        earlier = (
            (home_store[..., :, None] == home_store[..., None, :])
            & used_mask[..., None, :]
            & (entries[None, :] < entries[:, None])
        )
        rank = jnp.sum(earlier.astype(jnp.int32), axis=-1)
        match = (
            (home_store[None, :, :, None, :] == store_ids)
            & (rank[None, :, :, None, :] == slot_ids)
            & used_mask[None, :, :, None, :]
        )
        wanted = jnp.sum(jnp.where(match, home_slot[None, :, :, None, :] + 1, 0), axis=4) - 1
        received_ids = lax.all_to_all(wanted, "req", split_axis=0, concat_axis=0, tiled=True)
        served = kv_pool[layer_no][jnp.maximum(received_ids, 0), head_index]
        fetched = lax.all_to_all(served, "req", split_axis=0, concat_axis=0, tiled=True)
        spread = jnp.broadcast_to(queries[None], (n_req,) + queries.shape)
        stats = block_stats(spread, fetched, wanted >= 0)
        overall, denominator, numerator = combine(stats[0], stats[1], stats[2], (0, 4))
        context = (numerator / denominator[..., None]).astype(jnp.bfloat16).reshape(req_dev, -1)
        attn_part = jnp.dot(
            lax.all_gather(context, "req", axis=0, tiled=True),
            o_weight[layer_no],
            preferred_element_type=jnp.float32,
        )
        attended = (current.astype(jnp.float32) + sum_over_heads(attn_part)).astype(jnp.bfloat16)
        scaled = apply_gain(attended, ffn_gain[layer_no])
        inv_all = summed_inverse(attended)
        gate = jnp.dot(scaled, gate_weight[layer_no], preferred_element_type=jnp.float32)
        up_part = jnp.dot(scaled, up_weight[layer_no], preferred_element_type=jnp.float32)
        payload = (gate, up_part)
        totals = lax.psum((payload[0], payload[1]), "req")
        gate = totals[0] * inv_all[:, None]
        up_part = totals[1] * inv_all[:, None]
        activated = (jax.nn.silu(gate) * up_part).astype(jnp.bfloat16)
        ffn_part = jnp.dot(activated, down_weight[layer_no], preferred_element_type=jnp.float32)
        current = (attended.astype(jnp.float32) + sum_over_heads(ffn_part)).astype(jnp.bfloat16)
    return current


def decoder_kernel(
    n,
    nt,
    hidden_ref,
    attn_gain_ref,
    ffn_gain_ref,
    used_ref,
    turn_ref,
    q_hbm,
    o_hbm,
    gate_hbm,
    up_hbm,
    down_hbm,
    kv_hbm,
    out_ref,
    state,
    q_w,
    o_w,
    gate_w,
    up_w,
    down_w,
    kv_w,
    used_all,
    q_out,
    q_in,
    q_all,
    scores,
    part_out,
    part_in,
    ctx_all,
    ffn_out,
    ffn_in,
    act_all,
    head_sums,
    load_sem,
    send_sem,
    recv_sem,
    tp_send_sem,
    tp_recv_sem,
):
    me = lax.axis_index("req")
    my_tp = lax.axis_index("tp")
    hd = LANES
    slots = kv_w.shape[1]

    def load(layer, which):
        source, target = (
            (q_hbm, q_w),
            (kv_hbm, kv_w),
            (o_hbm, o_w),
            (gate_hbm, gate_w),
            (up_hbm, up_w),
            (down_hbm, down_w),
        )[which]
        if which == 1:
            source = source.at[layer, :, 0]
        else:
            source = source.at[layer]
        return pltpu.make_async_copy(source, target.at[layer], load_sem.at[layer, which])

    def peer(step):
        return lax.rem(me + step, n)

    def send(source, target, step, phase):
        return pltpu.make_async_remote_copy(
            src_ref=source,
            dst_ref=target,
            send_sem=send_sem.at[step],
            recv_sem=recv_sem.at[phase, me],
            device_id=(peer(step), my_tp),
            device_id_type=MESH,
        )

    def wait_from(slot, who, phase):
        pltpu.make_async_remote_copy(
            src_ref=slot,
            dst_ref=slot,
            send_sem=send_sem.at[0],
            recv_sem=recv_sem.at[phase, who],
            device_id=(who, my_tp),
            device_id_type=MESH,
        ).wait_recv()

    def exchange(source_of, target, phase):
        copies = [send(source_of(peer(step)), target.at[me], step, phase) for step in range(1, n)]
        for copy in copies:
            copy.start()
        return copies

    def finish(copies, target, phase):
        for step in range(1, n):
            who = peer(step)
            wait_from(target.at[who], who, phase)
        for copy in copies:
            copy.wait_send()

    def over_heads(buffer, phase):
        copies = []
        for step in range(1, nt):
            copies.append(
                pltpu.make_async_remote_copy(
                    src_ref=buffer.at[my_tp],
                    dst_ref=buffer.at[my_tp],
                    send_sem=tp_send_sem.at[step],
                    recv_sem=tp_recv_sem.at[phase, my_tp],
                    device_id=(me, lax.rem(my_tp + step, nt)),
                    device_id_type=MESH,
                )
            )
        for copy in copies:
            copy.start()
        for step in range(1, nt):
            who = lax.rem(my_tp + step, nt)
            pltpu.make_async_remote_copy(
                src_ref=buffer.at[who],
                dst_ref=buffer.at[who],
                send_sem=tp_send_sem.at[0],
                recv_sem=tp_recv_sem.at[phase, who],
                device_id=(me, who),
                device_id_type=MESH,
            ).wait_recv()
        for copy in copies:
            copy.wait_send()
        total = buffer[0]
        for index in range(1, nt):
            total = total + buffer[index]
        state[...] = (state[...] + total).astype(jnp.bfloat16).astype(jnp.float32)

    def normed(gain_ref, layer):
        current = state[...]
        gains = gain_ref[...].astype(jnp.float32)
        gain = jnp.where(layer == 0, gains[0:1], gains[1:2])
        squares = jnp.sum(current * current, axis=1, keepdims=True)
        return (current * gain).astype(jnp.bfloat16), jnp.broadcast_to(squares, (current.shape[0], LANES))

    def ffn_start(who):
        return pl.multiple_of((7 * who // 2) * LANES, LANES)

    for which in range(3):
        load(0, which).start()

    barrier = pltpu.get_barrier_semaphore()
    for step in range(1, n):
        pl.semaphore_signal(barrier, inc=1, device_id=(peer(step), my_tp), device_id_type=MESH)
    for step in range(1, nt):
        pl.semaphore_signal(
            barrier, inc=1, device_id=(me, lax.rem(my_tp + step, nt)), device_id_type=MESH
        )
    state[...] = hidden_ref[...].astype(jnp.float32)
    used_all[me] = used_ref[me]
    pl.semaphore_wait(barrier, n - 1 + nt - 1)

    used_phase = 6 * LAYERS
    used_copies = exchange(lambda who: used_ref.at[who], used_all, used_phase)
    finish(used_copies, used_all, used_phase)

    def layer_body(layer, carry):
        phase = 6 * layer
        scaled, squares = normed(attn_gain_ref, layer)
        load(layer, 0).wait()
        for pair in range(n // 2):
            product = jnp.dot(
                scaled,
                q_w[layer, :, pair * 2 * hd : (pair + 1) * 2 * hd],
                preferred_element_type=jnp.float32,
            )
            for half in range(2):
                q_out[2 * pair + half, 0:8] = product[:, half * hd : (half + 1) * hd]
                q_out[2 * pair + half, 8:16] = squares
        copies = exchange(lambda who: q_out.at[who], q_in.at[layer], phase)
        q_in[layer, me] = q_out[me]

        @pl.when(layer == 0)
        def _():
            for which in range(3, 6):
                load(0, which).start()

        finish(copies, q_in.at[layer], phase)
        total = q_in[layer, 0]
        for who in range(1, n):
            total = total + q_in[layer, who]
        query = total[0:8] * lax.rsqrt(total[8:16] / D + EPSILON)
        swapped = jnp.concatenate([query[:, hd // 2 :], query[:, : hd // 2]], axis=1)
        query = (query * turn_ref[0:8] + swapped * turn_ref[8:16]) * hd ** (-0.5)
        q_all[layer, me] = query.astype(jnp.bfloat16).astype(jnp.float32)
        copies = exchange(lambda who: q_all.at[layer, me], q_all.at[layer], phase + 1)
        rows8 = lax.broadcasted_iota(jnp.int32, (8, LANES), 0)
        used = jnp.zeros((8, LANES), jnp.float32)
        for who in range(n):
            used = jnp.where(rows8 == who, used_all[who, layer], used)
        load(layer, 1).wait()
        finish(copies, q_all.at[layer], phase + 1)

        queries = q_all[layer].reshape(n * 8, hd).astype(jnp.bfloat16)
        step_slots = TOKENS // LANES
        peak = jnp.full((n * 8, LANES), MASK_FILL, jnp.float32)
        for chunk in range(slots // step_slots):
            keys = kv_w[layer, chunk * step_slots : (chunk + 1) * step_slots, 0].reshape(TOKENS, hd)
            block = lax.dot_general(
                queries, keys, (((1,), (1,)), ((), ())), preferred_element_type=jnp.float32
            )
            for k in range(step_slots):
                slot = chunk * step_slots + k
                mask = jnp.broadcast_to(used[:, slot : slot + 1], (8, LANES)) > 0.5
                mask = jnp.broadcast_to(mask[None], (n, 8, LANES))
                piece = block[:, k * LANES : (k + 1) * LANES].reshape(n, 8, LANES)
                piece = jnp.where(mask, piece, MASK_FILL).reshape(n * 8, LANES)
                scores[:, slot * LANES : (slot + 1) * LANES] = piece
                peak = jnp.maximum(peak, piece)
        top = jnp.max(peak, axis=1, keepdims=True)
        sums = jnp.zeros((n * 8, LANES), jnp.float32)
        acc = jnp.zeros((n * 8, hd), jnp.float32)
        for chunk in range(slots // step_slots):
            terms = jnp.exp(scores[:, chunk * TOKENS : (chunk + 1) * TOKENS] - top)
            for k in range(step_slots):
                sums = sums + terms[:, k * LANES : (k + 1) * LANES]
            values = kv_w[layer, chunk * step_slots : (chunk + 1) * step_slots, 1].reshape(TOKENS, hd)
            acc = acc + jnp.dot(terms.astype(jnp.bfloat16), values, preferred_element_type=jnp.float32)
        total = jnp.sum(sums, axis=1, keepdims=True)
        lane = lax.broadcasted_iota(jnp.int32, (n * 8, LANES), 1)
        stats = jnp.where(lane < LANES // 2, top, total)
        for head in range(n):
            part_out[head, 0:8] = acc[head * 8 : (head + 1) * 8]
            part_out[head, 8:16] = stats[head * 8 : (head + 1) * 8]
        copies = exchange(lambda who: part_out.at[who], part_in.at[layer], phase + 2)
        part_in[layer, me] = part_out[me]
        finish(copies, part_in.at[layer], phase + 2)

        tops = [part_in[layer, who, 8:16][:, 0:1] for who in range(n)]
        overall = functools.reduce(jnp.maximum, tops)
        numerator = jnp.zeros((8, hd), jnp.float32)
        denominator = jnp.zeros((8, 1), jnp.float32)
        for who in range(n):
            rescale = jnp.exp(tops[who] - overall)
            numerator = numerator + rescale * part_in[layer, who, 0:8]
            denominator = denominator + rescale * part_in[layer, who, 8:16][:, LANES // 2 : LANES // 2 + 1]
        ctx_all[layer, me] = (numerator / denominator).astype(jnp.bfloat16).astype(jnp.float32)
        copies = exchange(lambda who: ctx_all.at[layer, me], ctx_all.at[layer], phase + 3)
        load(layer, 2).wait()
        finish(copies, ctx_all.at[layer], phase + 3)

        context = jnp.concatenate([ctx_all[layer, head] for head in range(n)], axis=1).astype(jnp.bfloat16)
        for part in range(n // 2):
            columns = slice(part * 256, (part + 1) * 256)
            head_sums[layer, 0, my_tp, :, columns] = jnp.dot(
                context, o_w[layer, :, columns], preferred_element_type=jnp.float32
            )
        over_heads(head_sums.at[layer, 0], 2 * layer)

        scaled, squares = normed(ffn_gain_ref, layer)
        load(layer, 3).wait()
        load(layer, 4).wait()

        def gate_up(who):
            columns = pl.ds(ffn_start(who), WIDE)
            ffn_out[who, :, 0:WIDE] = jnp.dot(
                scaled, gate_w[layer, :, columns], preferred_element_type=jnp.float32
            )
            ffn_out[who, :, WIDE : 2 * WIDE] = jnp.dot(
                scaled, up_w[layer, :, columns], preferred_element_type=jnp.float32
            )
            ffn_out[who, :, 2 * WIDE :] = squares

        def ffn_step(step, carry):
            who = peer(step)
            gate_up(who)
            send(ffn_out.at[who], ffn_in.at[layer, me], step, phase + 4).start()
            return carry

        lax.fori_loop(1, n, ffn_step, 0)

        @pl.when(layer + 1 < LAYERS)
        def _():
            for which in range(6):
                load(layer + 1, which).start()

        gate_up(me)
        ffn_in[layer, me] = ffn_out[me]
        copies = [send(ffn_out.at[peer(step)], ffn_in.at[layer, me], step, phase + 4) for step in range(1, n)]
        finish(copies, ffn_in.at[layer], phase + 4)
        total = ffn_in[layer, 0]
        for who in range(1, n):
            total = total + ffn_in[layer, who]
        inv = lax.rsqrt(total[:, 2 * WIDE :] / D + EPSILON)[:, 0:1]
        gate = total[:, 0:WIDE] * inv
        up = total[:, WIDE : 2 * WIDE] * inv
        act = gate / (1.0 + jnp.exp(-gate)) * up
        lane = lax.broadcasted_iota(jnp.int32, (8, WIDE), 1)
        act = jnp.where(lane < lax.rem(me, 2) * LANES, 0.0, act)
        packed = jnp.concatenate([act[:, 0 : WIDE // 2], act[:, WIDE // 2 :]], axis=0)
        act_all[layer, me] = packed.astype(jnp.bfloat16)
        copies = exchange(lambda who: act_all.at[layer, me], act_all.at[layer], phase + 5)
        load(layer, 5).wait()

        def down(who, total):
            packed = act_all[layer, who].astype(jnp.float32)
            act = jnp.concatenate([packed[0:8], packed[8:16]], axis=1).astype(jnp.bfloat16)
            return total + jnp.dot(
                act, down_w[layer, pl.ds(ffn_start(who), WIDE), :], preferred_element_type=jnp.float32
            )

        def down_step(step, total):
            who = lax.rem(me + n - step, n)
            wait_from(act_all.at[layer, who], who, phase + 5)
            return down(who, total)

        total = down(me, jnp.zeros(state.shape, jnp.float32))
        head_sums[layer, 1, my_tp] = lax.fori_loop(1, n, down_step, total)
        for copy in copies:
            copy.wait_send()
        over_heads(head_sums.at[layer, 1], 2 * layer + 1)
        return carry

    lax.fori_loop(0, LAYERS, layer_body, 0)
    out_ref[...] = state[...].astype(out_ref.dtype)


def rotary_table(head_size, position):
    freq = np.arange(head_size // 2, dtype=np.float64)
    angles = position * np.exp(freq * (-2.0 * math.log(500000.0) / head_size))
    cosine = np.concatenate([np.cos(angles), np.cos(angles)])
    sine = np.concatenate([-np.sin(angles), np.sin(angles)])
    table = np.concatenate([np.tile(cosine[None], (8, 1)), np.tile(sine[None], (8, 1))])
    return jnp.asarray(table, jnp.float32)


def used_slots(block_home, chosen, chosen_count, n, pool_dev):
    ctx = block_home.shape[1]
    entries = jnp.arange(chosen.shape[3])
    picked = (chosen[:, 0, 0, None, :] == jnp.arange(ctx)[None, :, None]) & (
        entries < chosen_count[:, 0, 0, None, None]
    )
    picked = jnp.any(picked, axis=2)
    local = jnp.arange(LANES)
    slot_ids = jnp.where(local < pool_dev, jnp.arange(n)[:, None] * pool_dev + local, -1)
    used = jnp.any(
        picked[None, :, :, None] & (block_home[0][None, None, :, None] == slot_ids[:, None, None, :]), axis=2
    )
    used = used.astype(jnp.float32)
    return jnp.broadcast_to(used[:, :, None, :], (n, used.shape[1], 8, LANES))


def fused_shards(
    n,
    nt,
    hidden,
    attn_gain,
    q_weight,
    o_weight,
    ffn_gain,
    gate_weight,
    up_weight,
    down_weight,
    kv_pool,
    block_home,
    chosen,
    chosen_count,
):
    pool_dev = kv_pool.shape[1]
    head_size = kv_pool.shape[5]
    requests, features = hidden.shape
    position = float(block_home.shape[1] * kv_pool.shape[4] - 1)
    used = used_slots(block_home, chosen, chosen_count, n, pool_dev)
    vmem = pl.BlockSpec(memory_space=pltpu.VMEM)
    anywhere = pl.BlockSpec(memory_space=pl.ANY)
    f32, bf16 = jnp.float32, jnp.bfloat16
    return pl.pallas_call(
        functools.partial(decoder_kernel, n, nt),
        out_shape=jax.ShapeDtypeStruct(hidden.shape, hidden.dtype),
        in_specs=[vmem] * 5 + [anywhere] * 6,
        out_specs=vmem,
        scratch_shapes=[
            pltpu.VMEM((requests, features), f32),
            pltpu.VMEM(q_weight.shape, bf16),
            pltpu.VMEM(o_weight.shape, bf16),
            pltpu.VMEM(gate_weight.shape, bf16),
            pltpu.VMEM(up_weight.shape, bf16),
            pltpu.VMEM(down_weight.shape, bf16),
            pltpu.VMEM(kv_pool.shape[:2] + kv_pool.shape[3:], bf16),
            pltpu.VMEM((n, LAYERS, 8, LANES), f32),
            pltpu.VMEM((n, 16, LANES), f32),
            pltpu.VMEM((LAYERS, n, 16, LANES), f32),
            pltpu.VMEM((LAYERS, n, 8, LANES), f32),
            pltpu.VMEM((8 * n, pool_dev * LANES), f32),
            pltpu.VMEM((n, 16, LANES), f32),
            pltpu.VMEM((LAYERS, n, 16, LANES), f32),
            pltpu.VMEM((LAYERS, n, 8, LANES), f32),
            pltpu.VMEM((n, 8, 2 * WIDE + LANES), f32),
            pltpu.VMEM((LAYERS, n, 8, 2 * WIDE + LANES), f32),
            pltpu.VMEM((LAYERS, n, 16, WIDE // 2), bf16),
            pltpu.VMEM((LAYERS, 2, nt, requests, features), f32),
            pltpu.SemaphoreType.DMA((LAYERS, 6)),
            pltpu.SemaphoreType.DMA((n,)),
            pltpu.SemaphoreType.DMA((6 * LAYERS + 1, n)),
            pltpu.SemaphoreType.DMA((nt,)),
            pltpu.SemaphoreType.DMA((2 * LAYERS, nt)),
        ],
        compiler_params=pltpu.CompilerParams(
            collective_id=0, has_side_effects=True, vmem_limit_bytes=62 * MIB
        ),
        name="decoder_layers",
    )(
        hidden,
        attn_gain,
        ffn_gain,
        used,
        rotary_table(head_size, position),
        q_weight,
        o_weight,
        gate_weight,
        up_weight,
        down_weight,
        kv_pool,
    )


def solution(mesh):
    n, nt = mesh.shape["req"], mesh.shape["tp"]
    body = functools.partial(fused_shards, n, nt) if n == 8 else shards
    return jax.shard_map(
        body,
        mesh=mesh,
        in_specs=(
            P(None, "req"),
            P(None, "req"),
            P(None, "req", "tp"),
            P(None, "tp", "req"),
            P(None, "req"),
            P(None, "req", "tp"),
            P(None, "req", "tp"),
            P(None, "tp", "req"),
            P(None, "req", "tp", None, None, None),
            P("req", None),
            P(None, "req", "tp", None),
            P(None, "req", "tp"),
        ),
        out_specs=P(None, "req"),
        check_vma=False,
    )
```

```python
import functools
import math

import jax
import jax.numpy as jnp
import numpy as np
from jax import lax
from jax.experimental import pallas as pl
from jax.experimental.pallas import tpu as pltpu
from jax.sharding import PartitionSpec as P

D = 8192
LAYERS = 2


MASK_FILL = -1e30
EPSILON = 1e-05
MESH = pl.DeviceIdType.MESH
LANES = 128
TOKENS = 512
WIDE = 512
PARTS = 2
MIB = 1 << 20


def rotary(queries, position):
    head_size = queries.shape[-1]
    half_size = head_size // 2
    freq_idx = jnp.arange(half_size).astype(queries.dtype)
    angles = position * jnp.exp(freq_idx * (-2.0 * math.log(500000.0) / head_size))
    cosine = jnp.cos(angles)
    sine_part = jnp.sin(angles)
    lower_half = queries[..., :half_size]
    upper_half = queries[..., half_size:]
    return jnp.concatenate(
        [
            lower_half * cosine - upper_half * sine_part,
            upper_half * cosine + lower_half * sine_part,
        ],
        axis=-1,
    )


def local_squares(current):
    widened = current.astype(jnp.float32)
    return jnp.sum(widened * widened, axis=1)


def apply_gain(current, gain):
    return (current.astype(jnp.float32) * gain.astype(jnp.float32)).astype(jnp.bfloat16)


def inverse_of(squares):
    return lax.rsqrt(squares / D + EPSILON)


def summed_inverse(current):
    return inverse_of(lax.psum(local_squares(current), "req"))


def sum_over_heads(partial_sum):
    return lax.psum(partial_sum, "tp")


def block_stats(queries, blocks, valid):
    scores = jnp.einsum(
        "sigeh,sigqbh->sigeqb", queries, blocks[:, :, :, :, 0], preferred_element_type=jnp.float32
    )
    block_max = jnp.max(scores, axis=5)
    exp_terms = jnp.exp(scores - block_max[..., None])
    block_sum = jnp.sum(exp_terms, axis=5)
    block_acc = jnp.einsum(
        "sigeqb,sigqbh->sigeqh",
        exp_terms.astype(jnp.bfloat16),
        blocks[:, :, :, :, 1],
        preferred_element_type=jnp.float32,
    )
    block_max = jnp.where(valid[:, :, :, None, :], block_max, MASK_FILL)
    return (block_max, block_sum, block_acc)


def combine(block_max, block_sum, block_acc, axes):
    overall = jnp.max(block_max, axis=axes, keepdims=True)
    rescale = jnp.exp(block_max - overall)
    numerator = jnp.sum(rescale[..., None] * block_acc, axis=axes)
    denominator = jnp.sum(rescale * block_sum, axis=axes)
    return (jnp.squeeze(overall, axes), denominator, numerator)


def shards(
    hidden,
    attn_gain,
    q_weight,
    o_weight,
    ffn_gain,
    gate_weight,
    up_weight,
    down_weight,
    kv_pool,
    block_home,
    chosen,
    chosen_count,
):
    n_req = lax.axis_size("req")
    req_dev = chosen.shape[1]
    heads_dev = chosen.shape[2]
    most_sel = chosen.shape[3]
    pool_dev = kv_pool.shape[1]
    head_size = kv_pool.shape[5]
    per_store = block_home.shape[1] // n_req
    position = float(block_home.shape[1] * kv_pool.shape[4] - 1)
    own_start = lax.axis_index("req") * req_dev
    row_index = jnp.arange(req_dev)[:, None, None]
    entries = jnp.arange(most_sel)
    store_ids = jnp.arange(n_req)[:, None, None, None, None]
    slot_ids = jnp.arange(per_store)[None, None, None, :, None]
    head_index = jnp.arange(heads_dev)[None, None, :, None]
    current = hidden
    for layer_no in range(LAYERS):
        scaled = apply_gain(current, attn_gain[layer_no])
        inv_all = summed_inverse(current)
        rows_in = scaled
        product = jnp.dot(rows_in, q_weight[layer_no], preferred_element_type=jnp.float32)
        summed = lax.psum_scatter(product, "req", scatter_dimension=0, tiled=True)
        inv_own = lax.dynamic_slice_in_dim(inv_all, own_start, req_dev, 0)
        queries = (summed * inv_own[:, None]).reshape(req_dev, heads_dev, -1, head_size)
        queries = (rotary(queries, position) * head_size ** (-0.5)).astype(jnp.bfloat16)
        pool_ids = block_home[row_index, chosen[layer_no]]
        home_store = pool_ids // pool_dev
        home_slot = pool_ids % pool_dev
        used_mask = entries[None, None, :] < chosen_count[layer_no][:, :, None]
        earlier = (
            (home_store[..., :, None] == home_store[..., None, :])
            & used_mask[..., None, :]
            & (entries[None, :] < entries[:, None])
        )
        rank = jnp.sum(earlier.astype(jnp.int32), axis=-1)
        match = (
            (home_store[None, :, :, None, :] == store_ids)
            & (rank[None, :, :, None, :] == slot_ids)
            & used_mask[None, :, :, None, :]
        )
        wanted = jnp.sum(jnp.where(match, home_slot[None, :, :, None, :] + 1, 0), axis=4) - 1
        received_ids = lax.all_to_all(wanted, "req", split_axis=0, concat_axis=0, tiled=True)
        served = kv_pool[layer_no][jnp.maximum(received_ids, 0), head_index]
        fetched = lax.all_to_all(served, "req", split_axis=0, concat_axis=0, tiled=True)
        spread = jnp.broadcast_to(queries[None], (n_req,) + queries.shape)
        stats = block_stats(spread, fetched, wanted >= 0)
        overall, denominator, numerator = combine(stats[0], stats[1], stats[2], (0, 4))
        context = (numerator / denominator[..., None]).astype(jnp.bfloat16).reshape(req_dev, -1)
        attn_part = jnp.dot(
            lax.all_gather(context, "req", axis=0, tiled=True),
            o_weight[layer_no],
            preferred_element_type=jnp.float32,
        )
        attended = (current.astype(jnp.float32) + sum_over_heads(attn_part)).astype(jnp.bfloat16)
        scaled = apply_gain(attended, ffn_gain[layer_no])
        inv_all = summed_inverse(attended)
        gate = jnp.dot(scaled, gate_weight[layer_no], preferred_element_type=jnp.float32)
        up_part = jnp.dot(scaled, up_weight[layer_no], preferred_element_type=jnp.float32)
        payload = (gate, up_part)
        totals = lax.psum((payload[0], payload[1]), "req")
        gate = totals[0] * inv_all[:, None]
        up_part = totals[1] * inv_all[:, None]
        activated = (jax.nn.silu(gate) * up_part).astype(jnp.bfloat16)
        ffn_part = jnp.dot(activated, down_weight[layer_no], preferred_element_type=jnp.float32)
        current = (attended.astype(jnp.float32) + sum_over_heads(ffn_part)).astype(jnp.bfloat16)
    return current


def decoder_kernel(
    n,
    nt,
    hidden_ref,
    attn_gain_ref,
    ffn_gain_ref,
    turn_ref,
    home_ref,
    chosen_ref,
    count_ref,
    q_hbm,
    o_hbm,
    gate_hbm,
    up_hbm,
    down_hbm,
    kv_hbm,
    out_ref,
    state,
    q_w,
    o_w,
    gate_w,
    up_w,
    down_w,
    kv_w,
    used_out,
    used_all,
    q_out,
    q_in,
    q_all,
    scores,
    part_out,
    part_in,
    ctx_all,
    ffn_out,
    ffn_in,
    act_all,
    head_sums,
    load_sem,
    send_sem,
    recv_sem,
    used_sem,
    tp_send_sem,
    tp_recv_sem,
):
    me = lax.axis_index("req")
    my_tp = lax.axis_index("tp")
    hd = LANES
    slots = kv_w.shape[1]

    def load(layer, which):
        source, target = (
            (q_hbm, q_w),
            (kv_hbm, kv_w),
            (o_hbm, o_w),
            (gate_hbm, gate_w),
            (up_hbm, up_w),
            (down_hbm, down_w),
        )[which]
        if which == 1:
            source = source.at[layer, :, 0]
        else:
            source = source.at[layer]
        return pltpu.make_async_copy(source, target.at[layer], load_sem.at[layer, which])

    def peer(step):
        return lax.rem(me + step, n)

    def send(source, target, step, phase):
        return pltpu.make_async_remote_copy(
            src_ref=source,
            dst_ref=target,
            send_sem=send_sem.at[step],
            recv_sem=recv_sem.at[phase, me],
            device_id=(peer(step), my_tp),
            device_id_type=MESH,
        )

    def wait_from(slot, who, phase):
        pltpu.make_async_remote_copy(
            src_ref=slot,
            dst_ref=slot,
            send_sem=send_sem.at[0],
            recv_sem=recv_sem.at[phase, who],
            device_id=(who, my_tp),
            device_id_type=MESH,
        ).wait_recv()

    def exchange(source_of, target, phase):
        copies = [send(source_of(peer(step)), target.at[me], step, phase) for step in range(1, n)]
        for copy in copies:
            copy.start()
        return copies

    def finish(copies, target, phase):
        for step in range(1, n):
            who = peer(step)
            wait_from(target.at[who], who, phase)
        for copy in copies:
            copy.wait_send()

    def head_copy(slot, step, phase, part, who):
        return pltpu.make_async_remote_copy(
            src_ref=slot,
            dst_ref=slot,
            send_sem=tp_send_sem.at[part, step],
            recv_sem=tp_recv_sem.at[phase, part, who],
            device_id=(me, lax.rem(my_tp + step, nt)),
            device_id_type=MESH,
        )

    def over_heads(product_of, buffer, phase):
        copies = []
        for part in range(PARTS):
            product = product_of(part)
            width = product.shape[1] // 2
            packed = jnp.concatenate([product[:, :width], product[:, width:]], axis=0)
            buffer[my_tp, part] = packed.astype(jnp.bfloat16)
            for step in range(nt - 1, 0, -1):
                copy = head_copy(buffer.at[my_tp, part], step, phase, part, my_tp)
                copy.start()
                copies.append(copy)
        for part in range(PARTS):
            for step in range(1, nt):
                who = lax.rem(my_tp + step, nt)
                head_copy(buffer.at[who, part], step, phase, part, who).wait_recv()
            total = buffer[0, part].astype(jnp.float32)
            for index in range(1, nt):
                total = total + buffer[index, part].astype(jnp.float32)
            total = jnp.concatenate([total[0:8], total[8:16]], axis=1)
            width = total.shape[1]
            columns = slice(part * width, (part + 1) * width)
            state[:, columns] = (state[:, columns] + total).astype(jnp.bfloat16).astype(jnp.float32)
        for copy in copies:
            copy.wait_send()

    def normed(gain_ref, layer):
        current = state[...]
        gains = gain_ref[...].astype(jnp.float32)
        gain = jnp.where(layer == 0, gains[0:1], gains[1:2])
        squares = jnp.sum(current * current, axis=1, keepdims=True)
        return (current * gain).astype(jnp.bfloat16), jnp.broadcast_to(squares, (current.shape[0], LANES))

    def ffn_start(who):
        return pl.multiple_of((7 * who // 2) * LANES, LANES)

    for which in range(3):
        load(0, which).start()

    barrier = pltpu.get_barrier_semaphore()
    for step in range(1, n):
        pl.semaphore_signal(barrier, inc=1, device_id=(peer(step), my_tp), device_id_type=MESH)
    for step in range(1, nt):
        pl.semaphore_signal(
            barrier, inc=1, device_id=(me, lax.rem(my_tp + step, nt)), device_id_type=MESH
        )
    state[...] = hidden_ref[...].astype(jnp.float32)

    def query_product(layer):
        scaled, squares = normed(attn_gain_ref, layer)
        load(layer, 0).wait()
        for pair in range(n // 2):
            product = jnp.dot(
                scaled,
                q_w[layer, :, pair * 2 * hd : (pair + 1) * 2 * hd],
                preferred_element_type=jnp.float32,
            )
            for half in range(2):
                q_out[2 * pair + half, 0:8] = product[:, half * hd : (half + 1) * hd]
                q_out[2 * pair + half, 8:16] = squares

    rows8 = lax.broadcasted_iota(jnp.int32, (n, LANES), 0)
    lanes8 = lax.broadcasted_iota(jnp.int32, (n, LANES), 1)
    slot_ids = jnp.where(lanes8 < slots, rows8 * slots + lanes8, -1)
    for layer in range(LAYERS):
        used = jnp.zeros((n, LANES), jnp.float32)
        for entry in range(chosen_ref.shape[3]):
            slot = home_ref[0, chosen_ref[layer, 0, 0, entry]]
            slot = jnp.where(entry < count_ref[layer, 0, 0], slot, -2)
            used = jnp.where(slot_ids == slot, 1.0, used)
        used_out[layer] = used
    query_product(0)
    for which in range(3, 6):
        load(0, which).start()
    pl.semaphore_wait(barrier, n - 1 + nt - 1)

    def used_copy(step):
        return pltpu.make_async_remote_copy(
            src_ref=used_out,
            dst_ref=used_all.at[me],
            send_sem=used_sem.at[step],
            recv_sem=recv_sem.at[6 * LAYERS, me],
            device_id=(peer(step), my_tp),
            device_id_type=MESH,
        )

    def layer_body(layer, carry):
        phase = 6 * layer
        copies = exchange(lambda who: q_out.at[who], q_in.at[layer], phase)
        q_in[layer, me] = q_out[me]

        @pl.when(layer == 0)
        def _():
            for step in range(1, n):
                used_copy(step).start()
            used_all[me] = used_out[...]

        finish(copies, q_in.at[layer], phase)
        total = q_in[layer, 0]
        for who in range(1, n):
            total = total + q_in[layer, who]
        query = total[0:8] * lax.rsqrt(total[8:16] / D + EPSILON)
        swapped = jnp.concatenate([query[:, hd // 2 :], query[:, : hd // 2]], axis=1)
        query = (query * turn_ref[0:8] + swapped * turn_ref[8:16]) * hd ** (-0.5)
        q_all[layer, me] = query.astype(jnp.bfloat16).astype(jnp.float32)
        copies = exchange(lambda who: q_all.at[layer, me], q_all.at[layer], phase + 1)

        @pl.when(layer == 0)
        def _():
            for step in range(1, n):
                wait_from(used_all.at[peer(step)], peer(step), 6 * LAYERS)
                used_copy(step).wait_send()

        used = jnp.zeros((8, LANES), jnp.float32)
        for who in range(n):
            row = jnp.where(rows8 == me, used_all[who, layer], 0.0)
            used = jnp.where(rows8 == who, jnp.sum(row, axis=0, keepdims=True), used)
        load(layer, 1).wait()
        finish(copies, q_all.at[layer], phase + 1)

        queries = q_all[layer].reshape(n * 8, hd).astype(jnp.bfloat16)
        step_slots = TOKENS // LANES
        peak = jnp.full((n * 8, LANES), MASK_FILL, jnp.float32)
        for chunk in range(slots // step_slots):
            keys = kv_w[layer, chunk * step_slots : (chunk + 1) * step_slots, 0].reshape(TOKENS, hd)
            block = lax.dot_general(
                queries, keys, (((1,), (1,)), ((), ())), preferred_element_type=jnp.float32
            )
            for k in range(step_slots):
                slot = chunk * step_slots + k
                mask = jnp.broadcast_to(used[:, slot : slot + 1], (8, LANES)) > 0.5
                mask = jnp.broadcast_to(mask[None], (n, 8, LANES))
                piece = block[:, k * LANES : (k + 1) * LANES].reshape(n, 8, LANES)
                piece = jnp.where(mask, piece, MASK_FILL).reshape(n * 8, LANES)
                scores[:, slot * LANES : (slot + 1) * LANES] = piece
                peak = jnp.maximum(peak, piece)
        top = jnp.max(peak, axis=1, keepdims=True)
        sums = jnp.zeros((n * 8, LANES), jnp.float32)
        acc = jnp.zeros((n * 8, hd), jnp.float32)
        for chunk in range(slots // step_slots):
            terms = jnp.exp(scores[:, chunk * TOKENS : (chunk + 1) * TOKENS] - top)
            for k in range(step_slots):
                sums = sums + terms[:, k * LANES : (k + 1) * LANES]
            values = kv_w[layer, chunk * step_slots : (chunk + 1) * step_slots, 1].reshape(TOKENS, hd)
            acc = acc + jnp.dot(terms.astype(jnp.bfloat16), values, preferred_element_type=jnp.float32)
        total = jnp.sum(sums, axis=1, keepdims=True)
        lane = lax.broadcasted_iota(jnp.int32, (n * 8, LANES), 1)
        stats = jnp.where(lane < LANES // 2, top, total)
        for head in range(n):
            part_out[head, 0:8] = acc[head * 8 : (head + 1) * 8]
            part_out[head, 8:16] = stats[head * 8 : (head + 1) * 8]
        copies = exchange(lambda who: part_out.at[who], part_in.at[layer], phase + 2)
        part_in[layer, me] = part_out[me]
        finish(copies, part_in.at[layer], phase + 2)

        tops = [part_in[layer, who, 8:16][:, 0:1] for who in range(n)]
        overall = functools.reduce(jnp.maximum, tops)
        numerator = jnp.zeros((8, hd), jnp.float32)
        denominator = jnp.zeros((8, 1), jnp.float32)
        for who in range(n):
            rescale = jnp.exp(tops[who] - overall)
            numerator = numerator + rescale * part_in[layer, who, 0:8]
            denominator = denominator + rescale * part_in[layer, who, 8:16][:, LANES // 2 : LANES // 2 + 1]
        ctx_all[layer, me] = (numerator / denominator).astype(jnp.bfloat16).astype(jnp.float32)
        copies = exchange(lambda who: ctx_all.at[layer, me], ctx_all.at[layer], phase + 3)
        load(layer, 2).wait()
        finish(copies, ctx_all.at[layer], phase + 3)

        context = jnp.concatenate([ctx_all[layer, head] for head in range(n)], axis=1).astype(jnp.bfloat16)
        width = state.shape[1] // PARTS

        def out_part(part):
            weight = o_w[layer, :, part * width : (part + 1) * width]
            return jnp.dot(context, weight, preferred_element_type=jnp.float32)

        over_heads(out_part, head_sums.at[layer, 0], 2 * layer)

        scaled, squares = normed(ffn_gain_ref, layer)
        load(layer, 3).wait()
        load(layer, 4).wait()

        def gate_up(who):
            columns = pl.ds(ffn_start(who), WIDE)
            ffn_out[who, :, 0:WIDE] = jnp.dot(
                scaled, gate_w[layer, :, columns], preferred_element_type=jnp.float32
            )
            ffn_out[who, :, WIDE : 2 * WIDE] = jnp.dot(
                scaled, up_w[layer, :, columns], preferred_element_type=jnp.float32
            )
            ffn_out[who, :, 2 * WIDE :] = squares

        def ffn_step(step, carry):
            who = peer(step)
            gate_up(who)
            send(ffn_out.at[who], ffn_in.at[layer, me], step, phase + 4).start()
            return carry

        lax.fori_loop(1, n, ffn_step, 0)

        @pl.when(layer + 1 < LAYERS)
        def _():
            for which in range(6):
                load(layer + 1, which).start()

        gate_up(me)
        ffn_in[layer, me] = ffn_out[me]
        copies = [send(ffn_out.at[peer(step)], ffn_in.at[layer, me], step, phase + 4) for step in range(1, n)]
        finish(copies, ffn_in.at[layer], phase + 4)
        total = ffn_in[layer, 0]
        for who in range(1, n):
            total = total + ffn_in[layer, who]
        inv = lax.rsqrt(total[:, 2 * WIDE :] / D + EPSILON)[:, 0:1]
        gate = total[:, 0:WIDE] * inv
        up = total[:, WIDE : 2 * WIDE] * inv
        act = gate / (1.0 + jnp.exp(-gate)) * up
        packed = jnp.concatenate([act[:, 0 : WIDE // 2], act[:, WIDE // 2 :]], axis=0)
        act_all[layer, me] = packed.astype(jnp.bfloat16)
        copies = exchange(lambda who: act_all.at[layer, me], act_all.at[layer], phase + 5)
        load(layer, 5).wait()

        finish(copies, act_all.at[layer], phase + 5)
        shares = []
        for who in range(n):
            packed = act_all[layer, who].astype(jnp.float32)
            share = jnp.concatenate([packed[0:8], packed[8:16]], axis=1)
            shares.append(share[:, (who % 2) * LANES :])
        act = jnp.concatenate(shares, axis=1).astype(jnp.bfloat16)

        def down_part(part):
            weight = down_w[layer, :, part * width : (part + 1) * width]
            return jnp.dot(act, weight, preferred_element_type=jnp.float32)

        over_heads(down_part, head_sums.at[layer, 1], 2 * layer + 1)

        @pl.when(layer + 1 < LAYERS)
        def _():
            query_product(layer + 1)

        return carry

    lax.fori_loop(0, LAYERS, layer_body, 0)
    out_ref[...] = state[...].astype(out_ref.dtype)


def rotary_table(head_size, position):
    freq = np.arange(head_size // 2, dtype=np.float64)
    angles = position * np.exp(freq * (-2.0 * math.log(500000.0) / head_size))
    cosine = np.concatenate([np.cos(angles), np.cos(angles)])
    sine = np.concatenate([-np.sin(angles), np.sin(angles)])
    table = np.concatenate([np.tile(cosine[None], (8, 1)), np.tile(sine[None], (8, 1))])
    return jnp.asarray(table, jnp.float32)


def fused_shards(
    n,
    nt,
    hidden,
    attn_gain,
    q_weight,
    o_weight,
    ffn_gain,
    gate_weight,
    up_weight,
    down_weight,
    kv_pool,
    block_home,
    chosen,
    chosen_count,
):
    pool_dev = kv_pool.shape[1]
    head_size = kv_pool.shape[5]
    requests, features = hidden.shape
    position = float(block_home.shape[1] * kv_pool.shape[4] - 1)
    vmem = pl.BlockSpec(memory_space=pltpu.VMEM)
    scalars = pl.BlockSpec(memory_space=pltpu.SMEM)
    anywhere = pl.BlockSpec(memory_space=pl.ANY)
    f32, bf16 = jnp.float32, jnp.bfloat16
    return pl.pallas_call(
        functools.partial(decoder_kernel, n, nt),
        out_shape=jax.ShapeDtypeStruct(hidden.shape, hidden.dtype),
        in_specs=[vmem] * 4 + [scalars] * 3 + [anywhere] * 6,
        out_specs=vmem,
        scratch_shapes=[
            pltpu.VMEM((requests, features), f32),
            pltpu.VMEM(q_weight.shape, bf16),
            pltpu.VMEM(o_weight.shape, bf16),
            pltpu.VMEM(gate_weight.shape, bf16),
            pltpu.VMEM(up_weight.shape, bf16),
            pltpu.VMEM(down_weight.shape, bf16),
            pltpu.VMEM(kv_pool.shape[:2] + kv_pool.shape[3:], bf16),
            pltpu.VMEM((LAYERS, n, LANES), f32),
            pltpu.VMEM((n, LAYERS, n, LANES), f32),
            pltpu.VMEM((n, 16, LANES), f32),
            pltpu.VMEM((LAYERS, n, 16, LANES), f32),
            pltpu.VMEM((LAYERS, n, 8, LANES), f32),
            pltpu.VMEM((8 * n, pool_dev * LANES), f32),
            pltpu.VMEM((n, 16, LANES), f32),
            pltpu.VMEM((LAYERS, n, 16, LANES), f32),
            pltpu.VMEM((LAYERS, n, 8, LANES), f32),
            pltpu.VMEM((n, 8, 2 * WIDE + LANES), f32),
            pltpu.VMEM((LAYERS, n, 8, 2 * WIDE + LANES), f32),
            pltpu.VMEM((LAYERS, n, 16, WIDE // 2), bf16),
            pltpu.VMEM((LAYERS, 2, nt, PARTS, 16, features // PARTS // 2), bf16),
            pltpu.SemaphoreType.DMA((LAYERS, 6)),
            pltpu.SemaphoreType.DMA((n,)),
            pltpu.SemaphoreType.DMA((6 * LAYERS + 1, n)),
            pltpu.SemaphoreType.DMA((n,)),
            pltpu.SemaphoreType.DMA((PARTS, nt)),
            pltpu.SemaphoreType.DMA((2 * LAYERS, PARTS, nt)),
        ],
        compiler_params=pltpu.CompilerParams(
            collective_id=0, has_side_effects=True, vmem_limit_bytes=62 * MIB
        ),
        name="decoder_layers",
    )(
        hidden,
        attn_gain,
        ffn_gain,
        rotary_table(head_size, position),
        block_home,
        chosen,
        chosen_count,
        q_weight,
        o_weight,
        gate_weight,
        up_weight,
        down_weight,
        kv_pool,
    )


def solution(mesh):
    n, nt = mesh.shape["req"], mesh.shape["tp"]
    body = functools.partial(fused_shards, n, nt) if n == 8 else shards
    return jax.shard_map(
        body,
        mesh=mesh,
        in_specs=(
            P(None, "req"),
            P(None, "req"),
            P(None, "req", "tp"),
            P(None, "tp", "req"),
            P(None, "req"),
            P(None, "req", "tp"),
            P(None, "req", "tp"),
            P(None, "tp", "req"),
            P(None, "req", "tp", None, None, None),
            P("req", None),
            P(None, "req", "tp", None),
            P(None, "req", "tp"),
        ),
        out_specs=P(None, "req"),
        check_vma=False,
    )
```

```python
import functools
import math

import jax
import jax.numpy as jnp
import numpy as np
from jax import lax
from jax.experimental import pallas as pl
from jax.experimental.pallas import tpu as pltpu
from jax.sharding import PartitionSpec as P

D = 8192
LAYERS = 2


MASK_FILL = -1e30
EPSILON = 1e-05
MESH = pl.DeviceIdType.MESH
LANES = 128
TOKENS = 512
WIDE = 512
PARTS = 2
PHASES = 5
MIB = 1 << 20


def rotary(queries, position):
    head_size = queries.shape[-1]
    half_size = head_size // 2
    freq_idx = jnp.arange(half_size).astype(queries.dtype)
    angles = position * jnp.exp(freq_idx * (-2.0 * math.log(500000.0) / head_size))
    cosine = jnp.cos(angles)
    sine_part = jnp.sin(angles)
    lower_half = queries[..., :half_size]
    upper_half = queries[..., half_size:]
    return jnp.concatenate(
        [
            lower_half * cosine - upper_half * sine_part,
            upper_half * cosine + lower_half * sine_part,
        ],
        axis=-1,
    )


def local_squares(current):
    widened = current.astype(jnp.float32)
    return jnp.sum(widened * widened, axis=1)


def apply_gain(current, gain):
    return (current.astype(jnp.float32) * gain.astype(jnp.float32)).astype(jnp.bfloat16)


def inverse_of(squares):
    return lax.rsqrt(squares / D + EPSILON)


def summed_inverse(current):
    return inverse_of(lax.psum(local_squares(current), "req"))


def sum_over_heads(partial_sum):
    return lax.psum(partial_sum, "tp")


def block_stats(queries, blocks, valid):
    scores = jnp.einsum(
        "sigeh,sigqbh->sigeqb", queries, blocks[:, :, :, :, 0], preferred_element_type=jnp.float32
    )
    block_max = jnp.max(scores, axis=5)
    exp_terms = jnp.exp(scores - block_max[..., None])
    block_sum = jnp.sum(exp_terms, axis=5)
    block_acc = jnp.einsum(
        "sigeqb,sigqbh->sigeqh",
        exp_terms.astype(jnp.bfloat16),
        blocks[:, :, :, :, 1],
        preferred_element_type=jnp.float32,
    )
    block_max = jnp.where(valid[:, :, :, None, :], block_max, MASK_FILL)
    return (block_max, block_sum, block_acc)


def combine(block_max, block_sum, block_acc, axes):
    overall = jnp.max(block_max, axis=axes, keepdims=True)
    rescale = jnp.exp(block_max - overall)
    numerator = jnp.sum(rescale[..., None] * block_acc, axis=axes)
    denominator = jnp.sum(rescale * block_sum, axis=axes)
    return (jnp.squeeze(overall, axes), denominator, numerator)


def shards(
    hidden,
    attn_gain,
    q_weight,
    o_weight,
    ffn_gain,
    gate_weight,
    up_weight,
    down_weight,
    kv_pool,
    block_home,
    chosen,
    chosen_count,
):
    n_req = lax.axis_size("req")
    req_dev = chosen.shape[1]
    heads_dev = chosen.shape[2]
    most_sel = chosen.shape[3]
    pool_dev = kv_pool.shape[1]
    head_size = kv_pool.shape[5]
    per_store = block_home.shape[1] // n_req
    position = float(block_home.shape[1] * kv_pool.shape[4] - 1)
    own_start = lax.axis_index("req") * req_dev
    row_index = jnp.arange(req_dev)[:, None, None]
    entries = jnp.arange(most_sel)
    store_ids = jnp.arange(n_req)[:, None, None, None, None]
    slot_ids = jnp.arange(per_store)[None, None, None, :, None]
    head_index = jnp.arange(heads_dev)[None, None, :, None]
    current = hidden
    for layer_no in range(LAYERS):
        scaled = apply_gain(current, attn_gain[layer_no])
        inv_all = summed_inverse(current)
        rows_in = scaled
        product = jnp.dot(rows_in, q_weight[layer_no], preferred_element_type=jnp.float32)
        summed = lax.psum_scatter(product, "req", scatter_dimension=0, tiled=True)
        inv_own = lax.dynamic_slice_in_dim(inv_all, own_start, req_dev, 0)
        queries = (summed * inv_own[:, None]).reshape(req_dev, heads_dev, -1, head_size)
        queries = (rotary(queries, position) * head_size ** (-0.5)).astype(jnp.bfloat16)
        pool_ids = block_home[row_index, chosen[layer_no]]
        home_store = pool_ids // pool_dev
        home_slot = pool_ids % pool_dev
        used_mask = entries[None, None, :] < chosen_count[layer_no][:, :, None]
        earlier = (
            (home_store[..., :, None] == home_store[..., None, :])
            & used_mask[..., None, :]
            & (entries[None, :] < entries[:, None])
        )
        rank = jnp.sum(earlier.astype(jnp.int32), axis=-1)
        match = (
            (home_store[None, :, :, None, :] == store_ids)
            & (rank[None, :, :, None, :] == slot_ids)
            & used_mask[None, :, :, None, :]
        )
        wanted = jnp.sum(jnp.where(match, home_slot[None, :, :, None, :] + 1, 0), axis=4) - 1
        received_ids = lax.all_to_all(wanted, "req", split_axis=0, concat_axis=0, tiled=True)
        served = kv_pool[layer_no][jnp.maximum(received_ids, 0), head_index]
        fetched = lax.all_to_all(served, "req", split_axis=0, concat_axis=0, tiled=True)
        spread = jnp.broadcast_to(queries[None], (n_req,) + queries.shape)
        stats = block_stats(spread, fetched, wanted >= 0)
        overall, denominator, numerator = combine(stats[0], stats[1], stats[2], (0, 4))
        context = (numerator / denominator[..., None]).astype(jnp.bfloat16).reshape(req_dev, -1)
        attn_part = jnp.dot(
            lax.all_gather(context, "req", axis=0, tiled=True),
            o_weight[layer_no],
            preferred_element_type=jnp.float32,
        )
        attended = (current.astype(jnp.float32) + sum_over_heads(attn_part)).astype(jnp.bfloat16)
        scaled = apply_gain(attended, ffn_gain[layer_no])
        inv_all = summed_inverse(attended)
        gate = jnp.dot(scaled, gate_weight[layer_no], preferred_element_type=jnp.float32)
        up_part = jnp.dot(scaled, up_weight[layer_no], preferred_element_type=jnp.float32)
        payload = (gate, up_part)
        totals = lax.psum((payload[0], payload[1]), "req")
        gate = totals[0] * inv_all[:, None]
        up_part = totals[1] * inv_all[:, None]
        activated = (jax.nn.silu(gate) * up_part).astype(jnp.bfloat16)
        ffn_part = jnp.dot(activated, down_weight[layer_no], preferred_element_type=jnp.float32)
        current = (attended.astype(jnp.float32) + sum_over_heads(ffn_part)).astype(jnp.bfloat16)
    return current


def decoder_kernel(
    n,
    nt,
    hidden_ref,
    attn_gain_ref,
    ffn_gain_ref,
    turn_ref,
    home_ref,
    chosen_ref,
    count_ref,
    q_hbm,
    o_hbm,
    gate_hbm,
    up_hbm,
    down_hbm,
    kv_hbm,
    out_ref,
    state,
    q_w,
    o_w,
    gate_w,
    up_w,
    down_w,
    kv_w,
    used_out,
    used_all,
    q_in,
    scores,
    part_in,
    ffn_out,
    ffn_in,
    act_all,
    head_sums,
    load_sem,
    send_sem,
    recv_sem,
    used_sem,
    q_send_sem,
    tp_send_sem,
    tp_recv_sem,
):
    me = lax.axis_index("req")
    my_tp = lax.axis_index("tp")
    hd = LANES
    order = [*range(2, n), 1]
    slots = kv_w.shape[1]

    def load(layer, which):
        source, target = (
            (q_hbm, q_w),
            (kv_hbm, kv_w),
            (o_hbm, o_w),
            (gate_hbm, gate_w),
            (up_hbm, up_w),
            (down_hbm, down_w),
        )[which]
        if which == 1:
            source = source.at[layer, :, 0]
        else:
            source = source.at[layer]
        return pltpu.make_async_copy(source, target.at[layer], load_sem.at[layer, which])

    def peer(step):
        return lax.rem(me + step, n)

    def send(source, target, step, phase):
        return pltpu.make_async_remote_copy(
            src_ref=source,
            dst_ref=target,
            send_sem=send_sem.at[step],
            recv_sem=recv_sem.at[phase, me],
            device_id=(peer(step), my_tp),
            device_id_type=MESH,
        )

    def wait_from(slot, who, phase):
        pltpu.make_async_remote_copy(
            src_ref=slot,
            dst_ref=slot,
            send_sem=send_sem.at[0],
            recv_sem=recv_sem.at[phase, who],
            device_id=(who, my_tp),
            device_id_type=MESH,
        ).wait_recv()

    def exchange(source_of, target, phase):
        copies = [send(source_of(peer(step)), target.at[me], step, phase) for step in order]
        for copy in copies:
            copy.start()
        return copies

    def finish(copies, target, phase):
        for step in range(1, n):
            who = peer(step)
            wait_from(target.at[who], who, phase)
        for copy in copies:
            copy.wait_send()

    def head_copy(slot, step, phase, part, who):
        return pltpu.make_async_remote_copy(
            src_ref=slot,
            dst_ref=slot,
            send_sem=tp_send_sem.at[part, step],
            recv_sem=tp_recv_sem.at[phase, part, who],
            device_id=(me, lax.rem(my_tp + step, nt)),
            device_id_type=MESH,
        )

    def over_heads(product_of, buffer, phase):
        copies = []
        for part in range(PARTS):
            product = product_of(part)
            width = product.shape[1] // 2
            packed = jnp.concatenate([product[:, :width], product[:, width:]], axis=0)
            buffer[my_tp, part] = packed.astype(jnp.bfloat16)
            for step in range(nt - 1, 0, -1):
                copy = head_copy(buffer.at[my_tp, part], step, phase, part, my_tp)
                copy.start()
                copies.append(copy)
        for part in range(PARTS):
            for step in range(1, nt):
                who = lax.rem(my_tp + step, nt)
                head_copy(buffer.at[who, part], step, phase, part, who).wait_recv()
            total = buffer[0, part].astype(jnp.float32)
            for index in range(1, nt):
                total = total + buffer[index, part].astype(jnp.float32)
            total = jnp.concatenate([total[0:8], total[8:16]], axis=1)
            width = total.shape[1]
            columns = slice(part * width, (part + 1) * width)
            state[:, columns] = (state[:, columns] + total).astype(jnp.bfloat16).astype(jnp.float32)
        for copy in copies:
            copy.wait_send()

    def normed(gain_ref, layer):
        current = state[...]
        gains = gain_ref[...].astype(jnp.float32)
        gain = jnp.where(layer == 0, gains[0:1], gains[1:2])
        squares = jnp.sum(current * current, axis=1, keepdims=True)
        return (current * gain).astype(jnp.bfloat16), jnp.broadcast_to(squares, (current.shape[0], LANES))

    def ffn_start(who):
        return pl.multiple_of((7 * who // 2) * LANES, LANES)

    for which in range(3):
        load(0, which).start()

    barrier = pltpu.get_barrier_semaphore()
    for step in range(1, n):
        pl.semaphore_signal(barrier, inc=1, device_id=(peer(step), my_tp), device_id_type=MESH)
    for step in range(1, nt):
        pl.semaphore_signal(
            barrier, inc=1, device_id=(me, lax.rem(my_tp + step, nt)), device_id_type=MESH
        )
    state[...] = hidden_ref[...].astype(jnp.float32)

    def query_copies(layer, part):
        return [
            pltpu.make_async_remote_copy(
                src_ref=q_in.at[layer, me, part],
                dst_ref=q_in.at[layer, me, part],
                send_sem=q_send_sem.at[part, step],
                recv_sem=recv_sem.at[PHASES * layer + part, me],
                device_id=(peer(step), my_tp),
                device_id_type=MESH,
            )
            for step in order
        ]

    def query_product(layer, sending):
        scaled, squares = normed(attn_gain_ref, layer)
        load(layer, 0).wait()
        high = squares.astype(jnp.bfloat16).astype(jnp.float32)
        tail = jnp.concatenate([high, squares - high], axis=0)
        width = q_w.shape[2] // PARTS
        for part in range(PARTS):
            product = jnp.dot(
                scaled,
                q_w[layer, :, part * width : (part + 1) * width],
                preferred_element_type=jnp.float32,
            )
            packed = jnp.concatenate([product[:, : width // 2], product[:, width // 2 :]], axis=0)
            q_in[layer, me, part] = jnp.concatenate([packed, tail], axis=1).astype(jnp.bfloat16)
            if sending:
                for copy in query_copies(layer, part):
                    copy.start()

    rows8 = lax.broadcasted_iota(jnp.int32, (n, LANES), 0)
    lanes8 = lax.broadcasted_iota(jnp.int32, (n, LANES), 1)
    slot_ids = jnp.where(lanes8 < slots, rows8 * slots + lanes8, -1)
    for layer in range(LAYERS):
        used = jnp.zeros((n, LANES), jnp.float32)
        for entry in range(chosen_ref.shape[3]):
            slot = home_ref[0, chosen_ref[layer, 0, 0, entry]]
            slot = jnp.where(entry < count_ref[0, 0, layer], slot, -2)
            used = jnp.where(slot_ids == slot, 1.0, used)
        used_out[layer] = used
    query_product(0, False)
    for which in range(3, 6):
        load(0, which).start()
    pl.semaphore_wait(barrier, n - 1 + nt - 1)

    def used_copy(step):
        return pltpu.make_async_remote_copy(
            src_ref=used_out,
            dst_ref=used_all.at[me],
            send_sem=used_sem.at[step],
            recv_sem=recv_sem.at[PHASES * LAYERS, me],
            device_id=(peer(step), my_tp),
            device_id_type=MESH,
        )

    for part in range(PARTS):
        for copy in query_copies(0, part):
            copy.start()
    for step in order:
        used_copy(step).start()
    used_all[me] = used_out[...]

    def layer_body(layer, carry):
        phase = PHASES * layer
        load(layer, 1).wait()

        @pl.when(layer == 0)
        def _():
            for step in range(1, n):
                wait_from(used_all.at[peer(step)], peer(step), PHASES * LAYERS)
                used_copy(step).wait_send()

        used = jnp.zeros((8, LANES), jnp.float32)
        for who in range(n):
            row = jnp.where(rows8 == me, used_all[who, layer], 0.0)
            used = jnp.where(rows8 == who, jnp.sum(row, axis=0, keepdims=True), used)
        heads = []
        for part in range(PARTS):
            for step in range(1, n):
                who = peer(step)
                wait_from(q_in.at[layer, who, part], who, phase + part)
            total = q_in[layer, 0, part].astype(jnp.float32)
            for who in range(1, n):
                total = total + q_in[layer, who, part].astype(jnp.float32)
            width = total.shape[1] - LANES
            squares = total[0:8, width:] + total[8:16, width:]
            inv = lax.rsqrt(squares / D + EPSILON)
            for half in range(2):
                for head in range(width // hd):
                    heads.append(total[half * 8 : half * 8 + 8, head * hd : (head + 1) * hd] * inv)
        queries = []
        for query in heads:
            swapped = jnp.concatenate([query[:, hd // 2 :], query[:, : hd // 2]], axis=1)
            queries.append((query * turn_ref[0:8] + swapped * turn_ref[8:16]) * hd ** (-0.5))
        queries = jnp.concatenate(queries, axis=0).astype(jnp.bfloat16)
        for part in range(PARTS):
            for copy in query_copies(layer, part):
                copy.wait_send()

        step_slots = TOKENS // LANES
        peak = jnp.full((n * 8, LANES), MASK_FILL, jnp.float32)
        for chunk in range(slots // step_slots):
            keys = kv_w[layer, chunk * step_slots : (chunk + 1) * step_slots, 0].reshape(TOKENS, hd)
            block = lax.dot_general(
                queries, keys, (((1,), (1,)), ((), ())), preferred_element_type=jnp.float32
            )
            for k in range(step_slots):
                slot = chunk * step_slots + k
                mask = jnp.broadcast_to(used[:, slot : slot + 1], (8, LANES)) > 0.5
                mask = jnp.broadcast_to(mask[None], (n, 8, LANES))
                piece = block[:, k * LANES : (k + 1) * LANES].reshape(n, 8, LANES)
                piece = jnp.where(mask, piece, MASK_FILL).reshape(n * 8, LANES)
                scores[:, slot * LANES : (slot + 1) * LANES] = piece
                peak = jnp.maximum(peak, piece)
        top = jnp.max(peak, axis=1, keepdims=True)
        sums = jnp.zeros((n * 8, LANES), jnp.float32)
        acc = jnp.zeros((n * 8, hd), jnp.float32)
        for chunk in range(slots // step_slots):
            terms = jnp.exp(scores[:, chunk * TOKENS : (chunk + 1) * TOKENS] - top)
            for k in range(step_slots):
                sums = sums + terms[:, k * LANES : (k + 1) * LANES]
            values = kv_w[layer, chunk * step_slots : (chunk + 1) * step_slots, 1].reshape(TOKENS, hd)
            acc = acc + jnp.dot(terms.astype(jnp.bfloat16), values, preferred_element_type=jnp.float32)
        total = jnp.sum(sums, axis=1, keepdims=True)
        level = top + jnp.log(total)
        stats = jnp.zeros((8, LANES), jnp.float32)
        lane = lax.broadcasted_iota(jnp.int32, (8, LANES), 1)
        for head in range(n):
            stats = jnp.where(lane == head, level[head * 8 : (head + 1) * 8], stats)
        high = stats.astype(jnp.bfloat16).astype(jnp.float32)
        payload = jnp.concatenate([acc / total, high, stats - high], axis=0)
        part_in[layer, me] = payload.astype(jnp.bfloat16)
        copies = exchange(lambda who: part_in.at[layer, me], part_in.at[layer], phase + 2)
        load(layer, 2).wait()
        finish(copies, part_in.at[layer], phase + 2)

        rows = 8 * n
        levels = []
        for who in range(n):
            pair = part_in[layer, who, rows : rows + 16].astype(jnp.float32)
            levels.append(pair[0:8] + pair[8:16])
        overall = functools.reduce(jnp.maximum, levels)
        shares = [jnp.exp(level - overall) for level in levels]
        denominator = functools.reduce(jnp.add, shares)
        context = [jnp.zeros((8, hd), jnp.float32) for _ in range(n)]
        for who in range(n):
            share = shares[who] / denominator
            parts = part_in[layer, who, 0:rows].astype(jnp.float32)
            for head in range(n):
                context[head] = context[head] + share[:, head : head + 1] * parts[head * 8 : (head + 1) * 8]
        context = jnp.concatenate(context, axis=1).astype(jnp.bfloat16)

        width = state.shape[1] // PARTS

        def out_part(part):
            weight = o_w[layer, :, part * width : (part + 1) * width]
            return jnp.dot(context, weight, preferred_element_type=jnp.float32)

        over_heads(out_part, head_sums.at[layer, 0], 2 * layer)

        scaled, squares = normed(ffn_gain_ref, layer)
        load(layer, 3).wait()
        load(layer, 4).wait()

        def gate_up(who):
            columns = pl.ds(ffn_start(who), WIDE)
            ffn_out[who, :, 0:WIDE] = jnp.dot(
                scaled, gate_w[layer, :, columns], preferred_element_type=jnp.float32
            )
            ffn_out[who, :, WIDE : 2 * WIDE] = jnp.dot(
                scaled, up_w[layer, :, columns], preferred_element_type=jnp.float32
            )
            ffn_out[who, :, 2 * WIDE :] = squares

        def ffn_step(step, carry):
            who = peer(step)
            gate_up(who)
            send(ffn_out.at[who], ffn_in.at[layer, me], step, phase + 3).start()
            return carry

        lax.fori_loop(1, n, ffn_step, 0)

        @pl.when(layer + 1 < LAYERS)
        def _():
            for which in range(6):
                load(layer + 1, which).start()

        gate_up(me)
        ffn_in[layer, me] = ffn_out[me]
        copies = [send(ffn_out.at[peer(step)], ffn_in.at[layer, me], step, phase + 3) for step in range(1, n)]
        finish(copies, ffn_in.at[layer], phase + 3)
        total = ffn_in[layer, 0]
        for who in range(1, n):
            total = total + ffn_in[layer, who]
        inv = lax.rsqrt(total[:, 2 * WIDE :] / D + EPSILON)[:, 0:1]
        gate = total[:, 0:WIDE] * inv
        up = total[:, WIDE : 2 * WIDE] * inv
        act = gate / (1.0 + jnp.exp(-gate)) * up
        packed = jnp.concatenate([act[:, 0 : WIDE // 2], act[:, WIDE // 2 :]], axis=0)
        act_all[layer, me] = packed.astype(jnp.bfloat16)
        copies = exchange(lambda who: act_all.at[layer, me], act_all.at[layer], phase + 4)
        load(layer, 5).wait()

        finish(copies, act_all.at[layer], phase + 4)
        shares = []
        for who in range(n):
            packed = act_all[layer, who].astype(jnp.float32)
            share = jnp.concatenate([packed[0:8], packed[8:16]], axis=1)
            shares.append(share[:, (who % 2) * LANES :])
        act = jnp.concatenate(shares, axis=1).astype(jnp.bfloat16)

        def down_part(part):
            weight = down_w[layer, :, part * width : (part + 1) * width]
            return jnp.dot(act, weight, preferred_element_type=jnp.float32)

        over_heads(down_part, head_sums.at[layer, 1], 2 * layer + 1)

        @pl.when(layer + 1 < LAYERS)
        def _():
            query_product(layer + 1, True)

        return carry

    lax.fori_loop(0, LAYERS, layer_body, 0)
    out_ref[...] = state[...].astype(out_ref.dtype)


def rotary_table(head_size, position):
    freq = np.arange(head_size // 2, dtype=np.float64)
    angles = position * np.exp(freq * (-2.0 * math.log(500000.0) / head_size))
    cosine = np.concatenate([np.cos(angles), np.cos(angles)])
    sine = np.concatenate([-np.sin(angles), np.sin(angles)])
    table = np.concatenate([np.tile(cosine[None], (8, 1)), np.tile(sine[None], (8, 1))])
    return jnp.asarray(table, jnp.float32)


def fused_shards(
    n,
    nt,
    hidden,
    attn_gain,
    q_weight,
    o_weight,
    ffn_gain,
    gate_weight,
    up_weight,
    down_weight,
    kv_pool,
    block_home,
    chosen,
    chosen_count,
):
    pool_dev = kv_pool.shape[1]
    head_size = kv_pool.shape[5]
    requests, features = hidden.shape
    position = float(block_home.shape[1] * kv_pool.shape[4] - 1)
    vmem = pl.BlockSpec(memory_space=pltpu.VMEM)
    scalars = pl.BlockSpec(memory_space=pltpu.SMEM)
    anywhere = pl.BlockSpec(memory_space=pl.ANY)
    f32, bf16 = jnp.float32, jnp.bfloat16
    return pl.pallas_call(
        functools.partial(decoder_kernel, n, nt),
        out_shape=jax.ShapeDtypeStruct(hidden.shape, hidden.dtype),
        in_specs=[vmem] * 4 + [scalars] * 3 + [anywhere] * 6,
        out_specs=vmem,
        scratch_shapes=[
            pltpu.VMEM((requests, features), f32),
            pltpu.VMEM(q_weight.shape, bf16),
            pltpu.VMEM(o_weight.shape, bf16),
            pltpu.VMEM(gate_weight.shape, bf16),
            pltpu.VMEM(up_weight.shape, bf16),
            pltpu.VMEM(down_weight.shape, bf16),
            pltpu.VMEM(kv_pool.shape[:2] + kv_pool.shape[3:], bf16),
            pltpu.VMEM((LAYERS, n, LANES), f32),
            pltpu.VMEM((n, LAYERS, n, LANES), f32),
            pltpu.VMEM((LAYERS, n, PARTS, 16, q_weight.shape[2] // PARTS // 2 + LANES), bf16),
            pltpu.VMEM((8 * n, pool_dev * LANES), f32),
            pltpu.VMEM((LAYERS, n, 8 * n + 16, LANES), bf16),
            pltpu.VMEM((n, 8, 2 * WIDE + LANES), f32),
            pltpu.VMEM((LAYERS, n, 8, 2 * WIDE + LANES), f32),
            pltpu.VMEM((LAYERS, n, 16, WIDE // 2), bf16),
            pltpu.VMEM((LAYERS, 2, nt, PARTS, 16, features // PARTS // 2), bf16),
            pltpu.SemaphoreType.DMA((LAYERS, 6)),
            pltpu.SemaphoreType.DMA((n,)),
            pltpu.SemaphoreType.DMA((PHASES * LAYERS + 1, n)),
            pltpu.SemaphoreType.DMA((n,)),
            pltpu.SemaphoreType.DMA((PARTS, n)),
            pltpu.SemaphoreType.DMA((PARTS, nt)),
            pltpu.SemaphoreType.DMA((2 * LAYERS, PARTS, nt)),
        ],
        compiler_params=pltpu.CompilerParams(
            collective_id=0, has_side_effects=True, vmem_limit_bytes=62 * MIB
        ),
        name="decoder_layers",
    )(
        hidden,
        attn_gain,
        ffn_gain,
        rotary_table(head_size, position),
        block_home,
        chosen,
        jnp.transpose(chosen_count, (1, 2, 0)),
        q_weight,
        o_weight,
        gate_weight,
        up_weight,
        down_weight,
        kv_pool,
    )


def solution(mesh):
    n, nt = mesh.shape["req"], mesh.shape["tp"]
    body = functools.partial(fused_shards, n, nt) if n == 8 else shards
    return jax.shard_map(
        body,
        mesh=mesh,
        in_specs=(
            P(None, "req"),
            P(None, "req"),
            P(None, "req", "tp"),
            P(None, "tp", "req"),
            P(None, "req"),
            P(None, "req", "tp"),
            P(None, "req", "tp"),
            P(None, "tp", "req"),
            P(None, "req", "tp", None, None, None),
            P("req", None),
            P(None, "req", "tp", None),
            P(None, "req", "tp"),
        ),
        out_specs=P(None, "req"),
        check_vma=False,
    )
```

```python
import functools
import math

import jax
import jax.numpy as jnp
import numpy as np
from jax import lax
from jax.experimental import pallas as pl
from jax.experimental.pallas import tpu as pltpu
from jax.sharding import PartitionSpec as P

D = 8192
LAYERS = 2


MASK_FILL = -1e30
EPSILON = 1e-05
MESH = pl.DeviceIdType.MESH
LANES = 128
TOKENS = 512
WIDE = 512
PARTS = 2
PHASES = 5
MIB = 1 << 20


def rotary(queries, position):
    head_size = queries.shape[-1]
    half_size = head_size // 2
    freq_idx = jnp.arange(half_size).astype(queries.dtype)
    angles = position * jnp.exp(freq_idx * (-2.0 * math.log(500000.0) / head_size))
    cosine = jnp.cos(angles)
    sine_part = jnp.sin(angles)
    lower_half = queries[..., :half_size]
    upper_half = queries[..., half_size:]
    return jnp.concatenate(
        [
            lower_half * cosine - upper_half * sine_part,
            upper_half * cosine + lower_half * sine_part,
        ],
        axis=-1,
    )


def local_squares(current):
    widened = current.astype(jnp.float32)
    return jnp.sum(widened * widened, axis=1)


def apply_gain(current, gain):
    return (current.astype(jnp.float32) * gain.astype(jnp.float32)).astype(jnp.bfloat16)


def inverse_of(squares):
    return lax.rsqrt(squares / D + EPSILON)


def summed_inverse(current):
    return inverse_of(lax.psum(local_squares(current), "req"))


def sum_over_heads(partial_sum):
    return lax.psum(partial_sum, "tp")


def block_stats(queries, blocks, valid):
    scores = jnp.einsum(
        "sigeh,sigqbh->sigeqb", queries, blocks[:, :, :, :, 0], preferred_element_type=jnp.float32
    )
    block_max = jnp.max(scores, axis=5)
    exp_terms = jnp.exp(scores - block_max[..., None])
    block_sum = jnp.sum(exp_terms, axis=5)
    block_acc = jnp.einsum(
        "sigeqb,sigqbh->sigeqh",
        exp_terms.astype(jnp.bfloat16),
        blocks[:, :, :, :, 1],
        preferred_element_type=jnp.float32,
    )
    block_max = jnp.where(valid[:, :, :, None, :], block_max, MASK_FILL)
    return (block_max, block_sum, block_acc)


def combine(block_max, block_sum, block_acc, axes):
    overall = jnp.max(block_max, axis=axes, keepdims=True)
    rescale = jnp.exp(block_max - overall)
    numerator = jnp.sum(rescale[..., None] * block_acc, axis=axes)
    denominator = jnp.sum(rescale * block_sum, axis=axes)
    return (jnp.squeeze(overall, axes), denominator, numerator)


def shards(
    hidden,
    attn_gain,
    q_weight,
    o_weight,
    ffn_gain,
    gate_weight,
    up_weight,
    down_weight,
    kv_pool,
    block_home,
    chosen,
    chosen_count,
):
    n_req = lax.axis_size("req")
    req_dev = chosen.shape[1]
    heads_dev = chosen.shape[2]
    most_sel = chosen.shape[3]
    pool_dev = kv_pool.shape[1]
    head_size = kv_pool.shape[5]
    per_store = block_home.shape[1] // n_req
    position = float(block_home.shape[1] * kv_pool.shape[4] - 1)
    own_start = lax.axis_index("req") * req_dev
    row_index = jnp.arange(req_dev)[:, None, None]
    entries = jnp.arange(most_sel)
    store_ids = jnp.arange(n_req)[:, None, None, None, None]
    slot_ids = jnp.arange(per_store)[None, None, None, :, None]
    head_index = jnp.arange(heads_dev)[None, None, :, None]
    current = hidden
    for layer_no in range(LAYERS):
        scaled = apply_gain(current, attn_gain[layer_no])
        inv_all = summed_inverse(current)
        rows_in = scaled
        product = jnp.dot(rows_in, q_weight[layer_no], preferred_element_type=jnp.float32)
        summed = lax.psum_scatter(product, "req", scatter_dimension=0, tiled=True)
        inv_own = lax.dynamic_slice_in_dim(inv_all, own_start, req_dev, 0)
        queries = (summed * inv_own[:, None]).reshape(req_dev, heads_dev, -1, head_size)
        queries = (rotary(queries, position) * head_size ** (-0.5)).astype(jnp.bfloat16)
        pool_ids = block_home[row_index, chosen[layer_no]]
        home_store = pool_ids // pool_dev
        home_slot = pool_ids % pool_dev
        used_mask = entries[None, None, :] < chosen_count[layer_no][:, :, None]
        earlier = (
            (home_store[..., :, None] == home_store[..., None, :])
            & used_mask[..., None, :]
            & (entries[None, :] < entries[:, None])
        )
        rank = jnp.sum(earlier.astype(jnp.int32), axis=-1)
        match = (
            (home_store[None, :, :, None, :] == store_ids)
            & (rank[None, :, :, None, :] == slot_ids)
            & used_mask[None, :, :, None, :]
        )
        wanted = jnp.sum(jnp.where(match, home_slot[None, :, :, None, :] + 1, 0), axis=4) - 1
        received_ids = lax.all_to_all(wanted, "req", split_axis=0, concat_axis=0, tiled=True)
        served = kv_pool[layer_no][jnp.maximum(received_ids, 0), head_index]
        fetched = lax.all_to_all(served, "req", split_axis=0, concat_axis=0, tiled=True)
        spread = jnp.broadcast_to(queries[None], (n_req,) + queries.shape)
        stats = block_stats(spread, fetched, wanted >= 0)
        overall, denominator, numerator = combine(stats[0], stats[1], stats[2], (0, 4))
        context = (numerator / denominator[..., None]).astype(jnp.bfloat16).reshape(req_dev, -1)
        attn_part = jnp.dot(
            lax.all_gather(context, "req", axis=0, tiled=True),
            o_weight[layer_no],
            preferred_element_type=jnp.float32,
        )
        attended = (current.astype(jnp.float32) + sum_over_heads(attn_part)).astype(jnp.bfloat16)
        scaled = apply_gain(attended, ffn_gain[layer_no])
        inv_all = summed_inverse(attended)
        gate = jnp.dot(scaled, gate_weight[layer_no], preferred_element_type=jnp.float32)
        up_part = jnp.dot(scaled, up_weight[layer_no], preferred_element_type=jnp.float32)
        payload = (gate, up_part)
        totals = lax.psum((payload[0], payload[1]), "req")
        gate = totals[0] * inv_all[:, None]
        up_part = totals[1] * inv_all[:, None]
        activated = (jax.nn.silu(gate) * up_part).astype(jnp.bfloat16)
        ffn_part = jnp.dot(activated, down_weight[layer_no], preferred_element_type=jnp.float32)
        current = (attended.astype(jnp.float32) + sum_over_heads(ffn_part)).astype(jnp.bfloat16)
    return current


def decoder_kernel(
    n,
    nt,
    hidden_ref,
    attn_gain_ref,
    ffn_gain_ref,
    turn_ref,
    home_ref,
    chosen_ref,
    count_ref,
    q_hbm,
    o_hbm,
    gate_hbm,
    up_hbm,
    down_hbm,
    kv_hbm,
    out_ref,
    state,
    q_w,
    o_w,
    gate_w,
    up_w,
    down_w,
    kv_w,
    used_out,
    used_all,
    q_in,
    scores,
    part_in,
    ffn_out,
    ffn_in,
    act_all,
    head_sums,
    load_sem,
    send_sem,
    recv_sem,
    used_sem,
    q_send_sem,
    tp_send_sem,
    tp_recv_sem,
):
    me = lax.axis_index("req")
    my_tp = lax.axis_index("tp")
    hd = LANES
    order = range(1, n)
    slots = kv_w.shape[1]

    def load(layer, which):
        source, target = (
            (q_hbm, q_w),
            (kv_hbm, kv_w),
            (o_hbm, o_w),
            (gate_hbm, gate_w),
            (up_hbm, up_w),
            (down_hbm, down_w),
        )[which]
        if which == 1:
            source = source.at[layer, :, 0]
        else:
            source = source.at[layer]
        return pltpu.make_async_copy(source, target.at[layer], load_sem.at[layer, which])

    def peer(step):
        kind = (step - 1) // 2
        row = (me // 4 + 1 - kind // 2) % 2
        column = (me // 2 + 1 - kind % 2) % 2
        return row * 4 + column * 2 + (me + step) % 2

    def send(source, target, step, phase):
        return pltpu.make_async_remote_copy(
            src_ref=source,
            dst_ref=target,
            send_sem=send_sem.at[step],
            recv_sem=recv_sem.at[phase, me],
            device_id=(peer(step), my_tp),
            device_id_type=MESH,
        )

    def wait_from(slot, who, phase):
        pltpu.make_async_remote_copy(
            src_ref=slot,
            dst_ref=slot,
            send_sem=send_sem.at[0],
            recv_sem=recv_sem.at[phase, who],
            device_id=(who, my_tp),
            device_id_type=MESH,
        ).wait_recv()

    def exchange(source_of, target, phase):
        copies = [send(source_of(peer(step)), target.at[me], step, phase) for step in order]
        for copy in copies:
            copy.start()
        return copies

    def finish(copies, target, phase):
        for copy in copies:
            copy.wait_send()
        for step in range(n - 1, 0, -1):
            who = peer(step)
            wait_from(target.at[who], who, phase)

    def head_copy(slot, step, phase, part, who):
        return pltpu.make_async_remote_copy(
            src_ref=slot,
            dst_ref=slot,
            send_sem=tp_send_sem.at[part, step],
            recv_sem=tp_recv_sem.at[phase, part, who],
            device_id=(me, lax.rem(my_tp + step, nt)),
            device_id_type=MESH,
        )

    def over_heads(product_of, buffer, phase):
        copies = []
        for part in range(PARTS):
            product = product_of(part)
            width = product.shape[1] // 2
            packed = jnp.concatenate([product[:, :width], product[:, width:]], axis=0)
            buffer[my_tp, part] = packed.astype(jnp.bfloat16)
            for step in range(1, nt):
                copy = head_copy(buffer.at[my_tp, part], step, phase, part, my_tp)
                copy.start()
                copies.append(copy)
        for copy in copies:
            copy.wait_send()
        for part in range(PARTS):
            for step in range(1, nt):
                who = lax.rem(my_tp + step, nt)
                head_copy(buffer.at[who, part], step, phase, part, who).wait_recv()
            total = buffer[0, part].astype(jnp.float32)
            for index in range(1, nt):
                total = total + buffer[index, part].astype(jnp.float32)
            total = jnp.concatenate([total[0:8], total[8:16]], axis=1)
            width = total.shape[1]
            columns = slice(part * width, (part + 1) * width)
            state[:, columns] = (state[:, columns] + total).astype(jnp.bfloat16).astype(jnp.float32)

    def normed(gain_ref, layer):
        current = state[...]
        gains = gain_ref[...].astype(jnp.float32)
        gain = jnp.where(layer == 0, gains[0:1], gains[1:2])
        squares = jnp.sum(current * current, axis=1, keepdims=True)
        return (current * gain).astype(jnp.bfloat16), jnp.broadcast_to(squares, (current.shape[0], LANES))

    def ffn_start(who):
        return pl.multiple_of((7 * who // 2) * LANES, LANES)

    for which in range(3):
        load(0, which).start()

    barrier = pltpu.get_barrier_semaphore()
    for step in range(1, n):
        pl.semaphore_signal(barrier, inc=1, device_id=(peer(step), my_tp), device_id_type=MESH)
    for step in range(1, nt):
        pl.semaphore_signal(
            barrier, inc=1, device_id=(me, lax.rem(my_tp + step, nt)), device_id_type=MESH
        )
    state[...] = hidden_ref[...].astype(jnp.float32)

    def query_copies(layer, part):
        return [
            pltpu.make_async_remote_copy(
                src_ref=q_in.at[layer, me, part],
                dst_ref=q_in.at[layer, me, part],
                send_sem=q_send_sem.at[part, step],
                recv_sem=recv_sem.at[PHASES * layer + part, me],
                device_id=(peer(step), my_tp),
                device_id_type=MESH,
            )
            for step in order
        ]

    def query_product(layer, sending):
        scaled, squares = normed(attn_gain_ref, layer)
        load(layer, 0).wait()
        high = squares.astype(jnp.bfloat16).astype(jnp.float32)
        tail = jnp.concatenate([high, squares - high], axis=0)
        width = q_w.shape[2] // PARTS
        for part in range(PARTS):
            product = jnp.dot(
                scaled,
                q_w[layer, :, part * width : (part + 1) * width],
                preferred_element_type=jnp.float32,
            )
            packed = jnp.concatenate([product[:, : width // 2], product[:, width // 2 :]], axis=0)
            q_in[layer, me, part] = jnp.concatenate([packed, tail], axis=1).astype(jnp.bfloat16)
            if sending:
                for copy in query_copies(layer, part):
                    copy.start()

    rows8 = lax.broadcasted_iota(jnp.int32, (n, LANES), 0)
    lanes8 = lax.broadcasted_iota(jnp.int32, (n, LANES), 1)
    slot_ids = jnp.where(lanes8 < slots, rows8 * slots + lanes8, -1)
    for layer in range(LAYERS):
        used = jnp.zeros((n, LANES), jnp.float32)
        for entry in range(chosen_ref.shape[3]):
            slot = home_ref[0, chosen_ref[layer, 0, 0, entry]]
            slot = jnp.where(entry < count_ref[0, 0, layer], slot, -2)
            used = jnp.where(slot_ids == slot, 1.0, used)
        used_out[layer] = used
    query_product(0, False)
    for which in (3, 4):
        load(0, which).start()
    pl.semaphore_wait(barrier, n - 1 + nt - 1)

    def used_copy(step):
        return pltpu.make_async_remote_copy(
            src_ref=used_out,
            dst_ref=used_all.at[me],
            send_sem=used_sem.at[step],
            recv_sem=recv_sem.at[PHASES * LAYERS, me],
            device_id=(peer(step), my_tp),
            device_id_type=MESH,
        )

    for part in range(PARTS):
        for copy in query_copies(0, part):
            copy.start()
    for step in order:
        used_copy(step).start()
    used_all[me] = used_out[...]

    def layer_body(layer, carry):
        phase = PHASES * layer
        load(layer, 1).wait()

        @pl.when(layer == 0)
        def _():
            for step in range(1, n):
                wait_from(used_all.at[peer(step)], peer(step), PHASES * LAYERS)
                used_copy(step).wait_send()

        used = jnp.zeros((8, LANES), jnp.float32)
        for who in range(n):
            row = jnp.where(rows8 == me, used_all[who, layer], 0.0)
            used = jnp.where(rows8 == who, jnp.sum(row, axis=0, keepdims=True), used)
        for part in range(PARTS):
            for copy in query_copies(layer, part):
                copy.wait_send()
        heads = []
        for part in range(PARTS):
            for step in range(n - 1, 0, -1):
                who = peer(step)
                wait_from(q_in.at[layer, who, part], who, phase + part)
            total = q_in[layer, 0, part].astype(jnp.float32)
            for who in range(1, n):
                total = total + q_in[layer, who, part].astype(jnp.float32)
            width = total.shape[1] - LANES
            squares = total[0:8, width:] + total[8:16, width:]
            inv = lax.rsqrt(squares / D + EPSILON)
            for half in range(2):
                for head in range(width // hd):
                    heads.append(total[half * 8 : half * 8 + 8, head * hd : (head + 1) * hd] * inv)
        queries = []
        for query in heads:
            swapped = jnp.concatenate([query[:, hd // 2 :], query[:, : hd // 2]], axis=1)
            queries.append((query * turn_ref[0:8] + swapped * turn_ref[8:16]) * hd ** (-0.5))
        queries = jnp.concatenate(queries, axis=0).astype(jnp.bfloat16)

        load(layer, 5).start()
        step_slots = TOKENS // LANES
        peak = jnp.full((n * 8, LANES), MASK_FILL, jnp.float32)
        for chunk in range(slots // step_slots):
            keys = kv_w[layer, chunk * step_slots : (chunk + 1) * step_slots, 0].reshape(TOKENS, hd)
            block = lax.dot_general(
                queries, keys, (((1,), (1,)), ((), ())), preferred_element_type=jnp.float32
            )
            for k in range(step_slots):
                slot = chunk * step_slots + k
                mask = jnp.broadcast_to(used[:, slot : slot + 1], (8, LANES)) > 0.5
                mask = jnp.broadcast_to(mask[None], (n, 8, LANES))
                piece = block[:, k * LANES : (k + 1) * LANES].reshape(n, 8, LANES)
                piece = jnp.where(mask, piece, MASK_FILL).reshape(n * 8, LANES)
                scores[:, slot * LANES : (slot + 1) * LANES] = piece
                peak = jnp.maximum(peak, piece)
        top = jnp.max(peak, axis=1, keepdims=True)
        sums = jnp.zeros((n * 8, LANES), jnp.float32)
        acc = jnp.zeros((n * 8, hd), jnp.float32)
        for chunk in range(slots // step_slots):
            terms = jnp.exp(scores[:, chunk * TOKENS : (chunk + 1) * TOKENS] - top)
            for k in range(step_slots):
                sums = sums + terms[:, k * LANES : (k + 1) * LANES]
            values = kv_w[layer, chunk * step_slots : (chunk + 1) * step_slots, 1].reshape(TOKENS, hd)
            acc = acc + jnp.dot(terms.astype(jnp.bfloat16), values, preferred_element_type=jnp.float32)
        total = jnp.sum(sums, axis=1, keepdims=True)
        level = top + jnp.log(total)
        stats = jnp.zeros((8, LANES), jnp.float32)
        lane = lax.broadcasted_iota(jnp.int32, (8, LANES), 1)
        for head in range(n):
            stats = jnp.where(lane == head, level[head * 8 : (head + 1) * 8], stats)
        high = stats.astype(jnp.bfloat16).astype(jnp.float32)
        payload = jnp.concatenate([acc / total, high, stats - high], axis=0)
        part_in[layer, me] = payload.astype(jnp.bfloat16)
        copies = exchange(lambda who: part_in.at[layer, me], part_in.at[layer], phase + 2)
        load(layer, 2).wait()
        finish(copies, part_in.at[layer], phase + 2)

        rows = 8 * n
        levels = []
        for who in range(n):
            pair = part_in[layer, who, rows : rows + 16].astype(jnp.float32)
            levels.append(pair[0:8] + pair[8:16])
        overall = functools.reduce(jnp.maximum, levels)
        shares = [jnp.exp(level - overall) for level in levels]
        denominator = functools.reduce(jnp.add, shares)
        context = [jnp.zeros((8, hd), jnp.float32) for _ in range(n)]
        for who in range(n):
            share = shares[who] / denominator
            parts = part_in[layer, who, 0:rows].astype(jnp.float32)
            for head in range(n):
                context[head] = context[head] + share[:, head : head + 1] * parts[head * 8 : (head + 1) * 8]
        context = jnp.concatenate(context, axis=1).astype(jnp.bfloat16)

        width = state.shape[1] // PARTS

        @pl.when(layer + 1 < LAYERS)
        def _():
            for which in (0, 1, 2):
                load(layer + 1, which).start()

        def out_part(part):
            weight = o_w[layer, :, part * width : (part + 1) * width]
            return jnp.dot(context, weight, preferred_element_type=jnp.float32)

        over_heads(out_part, head_sums.at[layer, 0], 2 * layer)

        scaled, squares = normed(ffn_gain_ref, layer)
        load(layer, 3).wait()
        load(layer, 4).wait()

        def gate_up(who):
            columns = pl.ds(ffn_start(who), WIDE)
            ffn_out[who, :, 0:WIDE] = jnp.dot(
                scaled, gate_w[layer, :, columns], preferred_element_type=jnp.float32
            )
            ffn_out[who, :, WIDE : 2 * WIDE] = jnp.dot(
                scaled, up_w[layer, :, columns], preferred_element_type=jnp.float32
            )
            ffn_out[who, :, 2 * WIDE :] = squares

        def ffn_step(step, carry):
            who = peer(step)
            gate_up(who)
            send(ffn_out.at[who], ffn_in.at[layer, me], step, phase + 3).start()
            return carry

        lax.fori_loop(1, n, ffn_step, 0)

        @pl.when(layer + 1 < LAYERS)
        def _():
            load(layer + 1, 3).start()

        gate_up(me)
        ffn_in[layer, me] = ffn_out[me]
        copies = [send(ffn_out.at[peer(step)], ffn_in.at[layer, me], step, phase + 3) for step in range(1, n)]
        finish(copies, ffn_in.at[layer], phase + 3)
        total = ffn_in[layer, 0]
        for who in range(1, n):
            total = total + ffn_in[layer, who]
        inv = lax.rsqrt(total[:, 2 * WIDE :] / D + EPSILON)[:, 0:1]
        gate = total[:, 0:WIDE] * inv
        up = total[:, WIDE : 2 * WIDE] * inv
        act = gate / (1.0 + jnp.exp(-gate)) * up
        packed = jnp.concatenate([act[:, 0 : WIDE // 2], act[:, WIDE // 2 :]], axis=0)
        act_all[layer, me] = packed.astype(jnp.bfloat16)
        copies = exchange(lambda who: act_all.at[layer, me], act_all.at[layer], phase + 4)
        load(layer, 5).wait()

        finish(copies, act_all.at[layer], phase + 4)
        shares = []
        for who in range(n):
            packed = act_all[layer, who].astype(jnp.float32)
            share = jnp.concatenate([packed[0:8], packed[8:16]], axis=1)
            shares.append(share[:, (who % 2) * LANES :])
        act = jnp.concatenate(shares, axis=1).astype(jnp.bfloat16)

        @pl.when(layer + 1 < LAYERS)
        def _():
            load(layer + 1, 4).start()

        def down_part(part):
            weight = down_w[layer, :, part * width : (part + 1) * width]
            return jnp.dot(act, weight, preferred_element_type=jnp.float32)

        over_heads(down_part, head_sums.at[layer, 1], 2 * layer + 1)

        @pl.when(layer + 1 < LAYERS)
        def _():
            query_product(layer + 1, True)

        return carry

    lax.fori_loop(0, LAYERS, layer_body, 0)
    out_ref[...] = state[...].astype(out_ref.dtype)


def rotary_table(head_size, position):
    freq = np.arange(head_size // 2, dtype=np.float64)
    angles = position * np.exp(freq * (-2.0 * math.log(500000.0) / head_size))
    cosine = np.concatenate([np.cos(angles), np.cos(angles)])
    sine = np.concatenate([-np.sin(angles), np.sin(angles)])
    table = np.concatenate([np.tile(cosine[None], (8, 1)), np.tile(sine[None], (8, 1))])
    return jnp.asarray(table, jnp.float32)


def fused_shards(
    n,
    nt,
    hidden,
    attn_gain,
    q_weight,
    o_weight,
    ffn_gain,
    gate_weight,
    up_weight,
    down_weight,
    kv_pool,
    block_home,
    chosen,
    chosen_count,
):
    pool_dev = kv_pool.shape[1]
    head_size = kv_pool.shape[5]
    requests, features = hidden.shape
    position = float(block_home.shape[1] * kv_pool.shape[4] - 1)
    vmem = pl.BlockSpec(memory_space=pltpu.VMEM)
    scalars = pl.BlockSpec(memory_space=pltpu.SMEM)
    anywhere = pl.BlockSpec(memory_space=pl.ANY)
    f32, bf16 = jnp.float32, jnp.bfloat16
    return pl.pallas_call(
        functools.partial(decoder_kernel, n, nt),
        out_shape=jax.ShapeDtypeStruct(hidden.shape, hidden.dtype),
        in_specs=[vmem] * 4 + [scalars] * 3 + [anywhere] * 6,
        out_specs=vmem,
        scratch_shapes=[
            pltpu.VMEM((requests, features), f32),
            pltpu.VMEM(q_weight.shape, bf16),
            pltpu.VMEM(o_weight.shape, bf16),
            pltpu.VMEM(gate_weight.shape, bf16),
            pltpu.VMEM(up_weight.shape, bf16),
            pltpu.VMEM(down_weight.shape, bf16),
            pltpu.VMEM(kv_pool.shape[:2] + kv_pool.shape[3:], bf16),
            pltpu.VMEM((LAYERS, n, LANES), f32),
            pltpu.VMEM((n, LAYERS, n, LANES), f32),
            pltpu.VMEM((LAYERS, n, PARTS, 16, q_weight.shape[2] // PARTS // 2 + LANES), bf16),
            pltpu.VMEM((8 * n, pool_dev * LANES), f32),
            pltpu.VMEM((LAYERS, n, 8 * n + 16, LANES), bf16),
            pltpu.VMEM((n, 8, 2 * WIDE + LANES), f32),
            pltpu.VMEM((LAYERS, n, 8, 2 * WIDE + LANES), f32),
            pltpu.VMEM((LAYERS, n, 16, WIDE // 2), bf16),
            pltpu.VMEM((LAYERS, 2, nt, PARTS, 16, features // PARTS // 2), bf16),
            pltpu.SemaphoreType.DMA((LAYERS, 6)),
            pltpu.SemaphoreType.DMA((n,)),
            pltpu.SemaphoreType.DMA((PHASES * LAYERS + 1, n)),
            pltpu.SemaphoreType.DMA((n,)),
            pltpu.SemaphoreType.DMA((PARTS, n)),
            pltpu.SemaphoreType.DMA((PARTS, nt)),
            pltpu.SemaphoreType.DMA((2 * LAYERS, PARTS, nt)),
        ],
        compiler_params=pltpu.CompilerParams(
            collective_id=0, has_side_effects=True, vmem_limit_bytes=62 * MIB
        ),
        name="decoder_layers",
    )(
        hidden,
        attn_gain,
        ffn_gain,
        rotary_table(head_size, position),
        block_home,
        chosen,
        jnp.transpose(chosen_count, (1, 2, 0)),
        q_weight,
        o_weight,
        gate_weight,
        up_weight,
        down_weight,
        kv_pool,
    )


def solution(mesh):
    n, nt = mesh.shape["req"], mesh.shape["tp"]
    body = functools.partial(fused_shards, n, nt) if n == 8 else shards
    return jax.shard_map(
        body,
        mesh=mesh,
        in_specs=(
            P(None, "req"),
            P(None, "req"),
            P(None, "req", "tp"),
            P(None, "tp", "req"),
            P(None, "req"),
            P(None, "req", "tp"),
            P(None, "req", "tp"),
            P(None, "tp", "req"),
            P(None, "req", "tp", None, None, None),
            P("req", None),
            P(None, "req", "tp", None),
            P(None, "req", "tp"),
        ),
        out_specs=P(None, "req"),
        check_vma=False,
    )
```

```python
import functools
import math

import jax
import jax.numpy as jnp
import numpy as np
from jax import lax
from jax.experimental import pallas as pl
from jax.experimental.pallas import tpu as pltpu
from jax.sharding import PartitionSpec as P

D = 8192
LAYERS = 2


MASK_FILL = -1e30
EPSILON = 1e-05
MESH = pl.DeviceIdType.MESH
LANES = 128
TOKENS = 512
WIDE = 512
CHIP_UNITS = 896
PARTS = 2
PHASES = 5
MIB = 1 << 20


def rotary(queries, position):
    head_size = queries.shape[-1]
    half_size = head_size // 2
    freq_idx = jnp.arange(half_size).astype(queries.dtype)
    angles = position * jnp.exp(freq_idx * (-2.0 * math.log(500000.0) / head_size))
    cosine = jnp.cos(angles)
    sine_part = jnp.sin(angles)
    lower_half = queries[..., :half_size]
    upper_half = queries[..., half_size:]
    return jnp.concatenate(
        [
            lower_half * cosine - upper_half * sine_part,
            upper_half * cosine + lower_half * sine_part,
        ],
        axis=-1,
    )


def local_squares(current):
    widened = current.astype(jnp.float32)
    return jnp.sum(widened * widened, axis=1)


def apply_gain(current, gain):
    return (current.astype(jnp.float32) * gain.astype(jnp.float32)).astype(jnp.bfloat16)


def inverse_of(squares):
    return lax.rsqrt(squares / D + EPSILON)


def summed_inverse(current):
    return inverse_of(lax.psum(local_squares(current), "req"))


def sum_over_heads(partial_sum):
    return lax.psum(partial_sum, "tp")


def block_stats(queries, blocks, valid):
    scores = jnp.einsum(
        "sigeh,sigqbh->sigeqb", queries, blocks[:, :, :, :, 0], preferred_element_type=jnp.float32
    )
    block_max = jnp.max(scores, axis=5)
    exp_terms = jnp.exp(scores - block_max[..., None])
    block_sum = jnp.sum(exp_terms, axis=5)
    block_acc = jnp.einsum(
        "sigeqb,sigqbh->sigeqh",
        exp_terms.astype(jnp.bfloat16),
        blocks[:, :, :, :, 1],
        preferred_element_type=jnp.float32,
    )
    block_max = jnp.where(valid[:, :, :, None, :], block_max, MASK_FILL)
    return (block_max, block_sum, block_acc)


def combine(block_max, block_sum, block_acc, axes):
    overall = jnp.max(block_max, axis=axes, keepdims=True)
    rescale = jnp.exp(block_max - overall)
    numerator = jnp.sum(rescale[..., None] * block_acc, axis=axes)
    denominator = jnp.sum(rescale * block_sum, axis=axes)
    return (jnp.squeeze(overall, axes), denominator, numerator)


def shards(
    hidden,
    attn_gain,
    q_weight,
    o_weight,
    ffn_gain,
    gate_weight,
    up_weight,
    down_weight,
    kv_pool,
    block_home,
    chosen,
    chosen_count,
):
    n_req = lax.axis_size("req")
    req_dev = chosen.shape[1]
    heads_dev = chosen.shape[2]
    most_sel = chosen.shape[3]
    pool_dev = kv_pool.shape[1]
    head_size = kv_pool.shape[5]
    per_store = block_home.shape[1] // n_req
    position = float(block_home.shape[1] * kv_pool.shape[4] - 1)
    own_start = lax.axis_index("req") * req_dev
    row_index = jnp.arange(req_dev)[:, None, None]
    entries = jnp.arange(most_sel)
    store_ids = jnp.arange(n_req)[:, None, None, None, None]
    slot_ids = jnp.arange(per_store)[None, None, None, :, None]
    head_index = jnp.arange(heads_dev)[None, None, :, None]
    current = hidden
    for layer_no in range(LAYERS):
        scaled = apply_gain(current, attn_gain[layer_no])
        inv_all = summed_inverse(current)
        rows_in = scaled
        product = jnp.dot(rows_in, q_weight[layer_no], preferred_element_type=jnp.float32)
        summed = lax.psum_scatter(product, "req", scatter_dimension=0, tiled=True)
        inv_own = lax.dynamic_slice_in_dim(inv_all, own_start, req_dev, 0)
        queries = (summed * inv_own[:, None]).reshape(req_dev, heads_dev, -1, head_size)
        queries = (rotary(queries, position) * head_size ** (-0.5)).astype(jnp.bfloat16)
        pool_ids = block_home[row_index, chosen[layer_no]]
        home_store = pool_ids // pool_dev
        home_slot = pool_ids % pool_dev
        used_mask = entries[None, None, :] < chosen_count[layer_no][:, :, None]
        earlier = (
            (home_store[..., :, None] == home_store[..., None, :])
            & used_mask[..., None, :]
            & (entries[None, :] < entries[:, None])
        )
        rank = jnp.sum(earlier.astype(jnp.int32), axis=-1)
        match = (
            (home_store[None, :, :, None, :] == store_ids)
            & (rank[None, :, :, None, :] == slot_ids)
            & used_mask[None, :, :, None, :]
        )
        wanted = jnp.sum(jnp.where(match, home_slot[None, :, :, None, :] + 1, 0), axis=4) - 1
        received_ids = lax.all_to_all(wanted, "req", split_axis=0, concat_axis=0, tiled=True)
        served = kv_pool[layer_no][jnp.maximum(received_ids, 0), head_index]
        fetched = lax.all_to_all(served, "req", split_axis=0, concat_axis=0, tiled=True)
        spread = jnp.broadcast_to(queries[None], (n_req,) + queries.shape)
        stats = block_stats(spread, fetched, wanted >= 0)
        overall, denominator, numerator = combine(stats[0], stats[1], stats[2], (0, 4))
        context = (numerator / denominator[..., None]).astype(jnp.bfloat16).reshape(req_dev, -1)
        attn_part = jnp.dot(
            lax.all_gather(context, "req", axis=0, tiled=True),
            o_weight[layer_no],
            preferred_element_type=jnp.float32,
        )
        attended = (current.astype(jnp.float32) + sum_over_heads(attn_part)).astype(jnp.bfloat16)
        scaled = apply_gain(attended, ffn_gain[layer_no])
        inv_all = summed_inverse(attended)
        gate = jnp.dot(scaled, gate_weight[layer_no], preferred_element_type=jnp.float32)
        up_part = jnp.dot(scaled, up_weight[layer_no], preferred_element_type=jnp.float32)
        payload = (gate, up_part)
        totals = lax.psum((payload[0], payload[1]), "req")
        gate = totals[0] * inv_all[:, None]
        up_part = totals[1] * inv_all[:, None]
        activated = (jax.nn.silu(gate) * up_part).astype(jnp.bfloat16)
        ffn_part = jnp.dot(activated, down_weight[layer_no], preferred_element_type=jnp.float32)
        current = (attended.astype(jnp.float32) + sum_over_heads(ffn_part)).astype(jnp.bfloat16)
    return current


def decoder_kernel(
    n,
    nt,
    hidden_ref,
    attn_gain_ref,
    ffn_gain_ref,
    turn_ref,
    home_ref,
    chosen_ref,
    count_ref,
    q_hbm,
    o_hbm,
    gate_hbm,
    up_hbm,
    down_hbm,
    kv_hbm,
    out_ref,
    state,
    q_w,
    o_w,
    gate_w,
    up_w,
    down_w,
    kv_w,
    used_out,
    used_all,
    q_in,
    scores,
    part_in,
    ffn_out,
    ffn_in,
    act_all,
    head_sums,
    load_sem,
    send_sem,
    recv_sem,
    used_sem,
    q_send_sem,
    tp_send_sem,
    tp_recv_sem,
):
    me = lax.axis_index("req")
    my_tp = lax.axis_index("tp")
    hd = LANES
    order = range(1, n)
    slots = kv_w.shape[1]

    def load(layer, which):
        source, target = (
            (q_hbm, q_w),
            (kv_hbm, kv_w),
            (o_hbm, o_w),
            (gate_hbm, gate_w),
            (up_hbm, up_w),
            (down_hbm, down_w),
        )[which]
        if which == 1:
            source = source.at[layer, :, 0]
        else:
            source = source.at[layer]
        return pltpu.make_async_copy(source, target.at[layer], load_sem.at[layer, which])

    def peer(step):
        kind = (step - 1) // 2
        row = (me // 4 + 1 - kind // 2) % 2
        column = (me // 2 + 1 - kind % 2) % 2
        return row * 4 + column * 2 + (me + step) % 2

    def send(source, target, step, phase):
        return pltpu.make_async_remote_copy(
            src_ref=source,
            dst_ref=target,
            send_sem=send_sem.at[step],
            recv_sem=recv_sem.at[phase, me],
            device_id=(peer(step), my_tp),
            device_id_type=MESH,
        )

    def wait_from(slot, who, phase):
        pltpu.make_async_remote_copy(
            src_ref=slot,
            dst_ref=slot,
            send_sem=send_sem.at[0],
            recv_sem=recv_sem.at[phase, who],
            device_id=(who, my_tp),
            device_id_type=MESH,
        ).wait_recv()

    def exchange(source_of, target, phase):
        copies = [send(source_of(peer(step)), target.at[me], step, phase) for step in order]
        for copy in copies:
            copy.start()
        return copies

    def finish(copies, target, phase):
        for copy in copies:
            copy.wait_send()
        for step in range(n - 1, 0, -1):
            who = peer(step)
            wait_from(target.at[who], who, phase)

    def head_copy(slot, step, phase, part, who):
        return pltpu.make_async_remote_copy(
            src_ref=slot,
            dst_ref=slot,
            send_sem=tp_send_sem.at[part, step],
            recv_sem=tp_recv_sem.at[phase, part, who],
            device_id=(me, lax.rem(my_tp + step, nt)),
            device_id_type=MESH,
        )

    def over_heads(product_of, buffer, phase):
        copies = []
        for part in range(PARTS):
            product = product_of(part)
            width = product.shape[1] // 2
            packed = jnp.concatenate([product[:, :width], product[:, width:]], axis=0)
            buffer[my_tp, part] = packed.astype(jnp.bfloat16)
            for step in range(1, nt):
                copy = head_copy(buffer.at[my_tp, part], step, phase, part, my_tp)
                copy.start()
                copies.append(copy)
        for copy in copies:
            copy.wait_send()
        for part in range(PARTS):
            for step in range(1, nt):
                who = lax.rem(my_tp + step, nt)
                head_copy(buffer.at[who, part], step, phase, part, who).wait_recv()
            total = buffer[0, part].astype(jnp.float32)
            for index in range(1, nt):
                total = total + buffer[index, part].astype(jnp.float32)
            total = jnp.concatenate([total[0:8], total[8:16]], axis=1)
            width = total.shape[1]
            columns = slice(part * width, (part + 1) * width)
            state[:, columns] = (state[:, columns] + total).astype(jnp.bfloat16).astype(jnp.float32)

    def normed(gain_ref, layer):
        current = state[...]
        gains = gain_ref[...].astype(jnp.float32)
        gain = jnp.where(layer == 0, gains[0:1], gains[1:2])
        squares = jnp.sum(current * current, axis=1, keepdims=True)
        return (current * gain).astype(jnp.bfloat16), jnp.broadcast_to(squares, (current.shape[0], LANES))

    def chip_units(chip):
        return pl.ds(pl.multiple_of(chip * CHIP_UNITS, LANES), CHIP_UNITS)

    for which in range(3):
        load(0, which).start()

    barrier = pltpu.get_barrier_semaphore()
    for step in range(1, n):
        pl.semaphore_signal(barrier, inc=1, device_id=(peer(step), my_tp), device_id_type=MESH)
    for step in range(1, nt):
        pl.semaphore_signal(
            barrier, inc=1, device_id=(me, lax.rem(my_tp + step, nt)), device_id_type=MESH
        )
    state[...] = hidden_ref[...].astype(jnp.float32)

    def query_copies(layer, part):
        return [
            pltpu.make_async_remote_copy(
                src_ref=q_in.at[layer, me, part],
                dst_ref=q_in.at[layer, me, part],
                send_sem=q_send_sem.at[part, step],
                recv_sem=recv_sem.at[PHASES * layer + part, me],
                device_id=(peer(step), my_tp),
                device_id_type=MESH,
            )
            for step in order
        ]

    def query_product(layer, sending):
        scaled, squares = normed(attn_gain_ref, layer)
        load(layer, 0).wait()
        high = squares.astype(jnp.bfloat16).astype(jnp.float32)
        tail = jnp.concatenate([high, squares - high], axis=0)
        width = q_w.shape[2] // PARTS
        for part in range(PARTS):
            product = jnp.dot(
                scaled,
                q_w[layer, :, part * width : (part + 1) * width],
                preferred_element_type=jnp.float32,
            )
            packed = jnp.concatenate([product[:, : width // 2], product[:, width // 2 :]], axis=0)
            q_in[layer, me, part] = jnp.concatenate([packed, tail], axis=1).astype(jnp.bfloat16)
            if sending:
                for copy in query_copies(layer, part):
                    copy.start()

    query_product(0, False)
    for which in (3, 4):
        load(0, which).start()
    pl.semaphore_wait(barrier, n - 1 + nt - 1)

    def used_copy(step):
        return pltpu.make_async_remote_copy(
            src_ref=used_out,
            dst_ref=used_all.at[me],
            send_sem=used_sem.at[step],
            recv_sem=recv_sem.at[PHASES * LAYERS, me],
            device_id=(peer(step), my_tp),
            device_id_type=MESH,
        )

    for part in range(PARTS):
        for copy in query_copies(0, part):
            copy.start()
    rows8 = lax.broadcasted_iota(jnp.int32, (n, LANES), 0)
    lanes8 = lax.broadcasted_iota(jnp.int32, (n, LANES), 1)
    slot_ids = jnp.where(lanes8 < slots, rows8 * slots + lanes8, -1)
    for layer in range(LAYERS):
        used = jnp.zeros((n, LANES), jnp.float32)
        for entry in range(chosen_ref.shape[3]):
            slot = home_ref[0, chosen_ref[layer, 0, 0, entry]]
            slot = jnp.where(entry < count_ref[0, 0, layer], slot, -2)
            used = jnp.where(slot_ids == slot, 1.0, used)
        used_out[layer] = used
    for step in order:
        used_copy(step).start()
    used_all[me] = used_out[...]

    def layer_body(layer, carry):
        phase = PHASES * layer
        load(layer, 1).wait()

        @pl.when(layer == 0)
        def _():
            for step in range(1, n):
                wait_from(used_all.at[peer(step)], peer(step), PHASES * LAYERS)
                used_copy(step).wait_send()

        used = jnp.zeros((8, LANES), jnp.float32)
        for who in range(n):
            row = jnp.where(rows8 == me, used_all[who, layer], 0.0)
            used = jnp.where(rows8 == who, jnp.sum(row, axis=0, keepdims=True), used)
        for part in range(PARTS):
            for copy in query_copies(layer, part):
                copy.wait_send()
        heads = []
        for part in range(PARTS):
            for step in range(n - 1, 0, -1):
                who = peer(step)
                wait_from(q_in.at[layer, who, part], who, phase + part)
            total = q_in[layer, 0, part].astype(jnp.float32)
            for who in range(1, n):
                total = total + q_in[layer, who, part].astype(jnp.float32)
            width = total.shape[1] - LANES
            squares = total[0:8, width:] + total[8:16, width:]
            inv = lax.rsqrt(squares / D + EPSILON)
            for half in range(2):
                for head in range(width // hd):
                    heads.append(total[half * 8 : half * 8 + 8, head * hd : (head + 1) * hd] * inv)
        queries = []
        for query in heads:
            swapped = jnp.concatenate([query[:, hd // 2 :], query[:, : hd // 2]], axis=1)
            queries.append((query * turn_ref[0:8] + swapped * turn_ref[8:16]) * hd ** (-0.5))
        queries = jnp.concatenate(queries, axis=0).astype(jnp.bfloat16)

        load(layer, 5).start()
        step_slots = TOKENS // LANES
        peak = jnp.full((n * 8, LANES), MASK_FILL, jnp.float32)
        for chunk in range(slots // step_slots):
            keys = kv_w[layer, chunk * step_slots : (chunk + 1) * step_slots, 0].reshape(TOKENS, hd)
            block = lax.dot_general(
                queries, keys, (((1,), (1,)), ((), ())), preferred_element_type=jnp.float32
            )
            for k in range(step_slots):
                slot = chunk * step_slots + k
                mask = jnp.broadcast_to(used[:, slot : slot + 1], (8, LANES)) > 0.5
                mask = jnp.broadcast_to(mask[None], (n, 8, LANES))
                piece = block[:, k * LANES : (k + 1) * LANES].reshape(n, 8, LANES)
                piece = jnp.where(mask, piece, MASK_FILL).reshape(n * 8, LANES)
                scores[:, slot * LANES : (slot + 1) * LANES] = piece
                peak = jnp.maximum(peak, piece)
        top = jnp.max(peak, axis=1, keepdims=True)
        sums = jnp.zeros((n * 8, LANES), jnp.float32)
        acc = jnp.zeros((n * 8, hd), jnp.float32)
        for chunk in range(slots // step_slots):
            terms = jnp.exp(scores[:, chunk * TOKENS : (chunk + 1) * TOKENS] - top)
            for k in range(step_slots):
                sums = sums + terms[:, k * LANES : (k + 1) * LANES]
            values = kv_w[layer, chunk * step_slots : (chunk + 1) * step_slots, 1].reshape(TOKENS, hd)
            acc = acc + jnp.dot(terms.astype(jnp.bfloat16), values, preferred_element_type=jnp.float32)
        total = jnp.sum(sums, axis=1, keepdims=True)
        level = top + jnp.log(total)
        stats = jnp.zeros((8, LANES), jnp.float32)
        lane = lax.broadcasted_iota(jnp.int32, (8, LANES), 1)
        for head in range(n):
            stats = jnp.where(lane == head, level[head * 8 : (head + 1) * 8], stats)
        high = stats.astype(jnp.bfloat16).astype(jnp.float32)
        payload = jnp.concatenate([acc / total, high, stats - high], axis=0)
        part_in[layer, me] = payload.astype(jnp.bfloat16)
        copies = exchange(lambda who: part_in.at[layer, me], part_in.at[layer], phase + 2)
        load(layer, 2).wait()
        finish(copies, part_in.at[layer], phase + 2)

        rows = 8 * n
        levels = []
        for who in range(n):
            pair = part_in[layer, who, rows : rows + 16].astype(jnp.float32)
            levels.append(pair[0:8] + pair[8:16])
        overall = functools.reduce(jnp.maximum, levels)
        shares = [jnp.exp(level - overall) for level in levels]
        denominator = functools.reduce(jnp.add, shares)
        context = [jnp.zeros((8, hd), jnp.float32) for _ in range(n)]
        for who in range(n):
            share = shares[who] / denominator
            parts = part_in[layer, who, 0:rows].astype(jnp.float32)
            for head in range(n):
                context[head] = context[head] + share[:, head : head + 1] * parts[head * 8 : (head + 1) * 8]
        context = jnp.concatenate(context, axis=1).astype(jnp.bfloat16)

        width = state.shape[1] // PARTS

        @pl.when(layer + 1 < LAYERS)
        def _():
            for which in (0, 1, 2):
                load(layer + 1, which).start()

        def out_part(part):
            weight = o_w[layer, :, part * width : (part + 1) * width]
            return jnp.dot(context, weight, preferred_element_type=jnp.float32)

        over_heads(out_part, head_sums.at[layer, 0], 2 * layer)

        scaled, squares = normed(ffn_gain_ref, layer)
        load(layer, 3).wait()
        load(layer, 4).wait()

        def gate_up(chip):
            for index, weight in enumerate((gate_w, up_w)):
                product = jnp.dot(scaled, weight[layer, :, chip_units(chip)], preferred_element_type=jnp.float32)
                columns = slice(index * WIDE, (index + 1) * WIDE)
                ffn_out[2 * chip, :, columns] = product[:, 0:WIDE]
                ffn_out[2 * chip + 1, :, columns] = product[:, CHIP_UNITS - WIDE :]
            ffn_out[2 * chip, :, 2 * WIDE :] = squares
            ffn_out[2 * chip + 1, :, 2 * WIDE :] = squares

        def ffn_send(step):
            return send(ffn_out.at[peer(step)], ffn_in.at[layer, me], step, phase + 3)

        def ffn_step(kind, carry):
            gate_up(peer(2 * kind + 1) // 2)
            ffn_send(2 * kind + 1).start()
            ffn_send(2 * kind + 2).start()
            return carry

        lax.fori_loop(0, n // 2 - 1, ffn_step, 0)

        @pl.when(layer + 1 < LAYERS)
        def _():
            load(layer + 1, 3).start()

        gate_up(me // 2)
        ffn_send(n - 1).start()
        ffn_in[layer, me] = ffn_out[me]
        copies = [ffn_send(step) for step in order]
        finish(copies, ffn_in.at[layer], phase + 3)
        total = ffn_in[layer, 0]
        for who in range(1, n):
            total = total + ffn_in[layer, who]
        inv = lax.rsqrt(total[:, 2 * WIDE :] / D + EPSILON)[:, 0:1]
        gate = total[:, 0:WIDE] * inv
        up = total[:, WIDE : 2 * WIDE] * inv
        act = gate / (1.0 + jnp.exp(-gate)) * up
        packed = jnp.concatenate([act[:, 0 : WIDE // 2], act[:, WIDE // 2 :]], axis=0)
        act_all[layer, me] = packed.astype(jnp.bfloat16)
        copies = exchange(lambda who: act_all.at[layer, me], act_all.at[layer], phase + 4)
        load(layer, 5).wait()

        def chip_act(chip):
            shares = []
            for core in range(2):
                packed = act_all[layer, 2 * chip + core].astype(jnp.float32)
                shares.append(jnp.concatenate([packed[0:8], packed[8:16]], axis=1))
            both = [shares[0], shares[1][:, 2 * WIDE - CHIP_UNITS :]]
            return jnp.concatenate(both, axis=1).astype(jnp.bfloat16)

        def arrived(step):
            wait_from(act_all.at[layer, peer(step)], peer(step), phase + 4)

        arrived(n - 1)
        sums = jnp.dot(
            chip_act(me // 2), down_w[layer, chip_units(me // 2), :], preferred_element_type=jnp.float32
        )
        for copy in copies:
            copy.wait_send()
        for kind in range(n // 2 - 2, 0, -1):
            arrived(2 * kind + 1)
            arrived(2 * kind + 2)
            chip = peer(2 * kind + 1) // 2
            sums = sums + jnp.dot(
                chip_act(chip), down_w[layer, chip_units(chip), :], preferred_element_type=jnp.float32
            )
        arrived(1)
        arrived(2)
        last = peer(1) // 2
        act = chip_act(last)

        @pl.when(layer + 1 < LAYERS)
        def _():
            load(layer + 1, 4).start()

        def down_part(part):
            columns = slice(part * width, (part + 1) * width)
            weight = down_w[layer, chip_units(last), columns]
            return sums[:, columns] + jnp.dot(act, weight, preferred_element_type=jnp.float32)

        over_heads(down_part, head_sums.at[layer, 1], 2 * layer + 1)

        @pl.when(layer + 1 < LAYERS)
        def _():
            query_product(layer + 1, True)

        return carry

    lax.fori_loop(0, LAYERS, layer_body, 0)
    out_ref[...] = state[...].astype(out_ref.dtype)


def rotary_table(head_size, position):
    freq = np.arange(head_size // 2, dtype=np.float64)
    angles = position * np.exp(freq * (-2.0 * math.log(500000.0) / head_size))
    cosine = np.concatenate([np.cos(angles), np.cos(angles)])
    sine = np.concatenate([-np.sin(angles), np.sin(angles)])
    table = np.concatenate([np.tile(cosine[None], (8, 1)), np.tile(sine[None], (8, 1))])
    return jnp.asarray(table, jnp.float32)


def fused_shards(
    n,
    nt,
    hidden,
    attn_gain,
    q_weight,
    o_weight,
    ffn_gain,
    gate_weight,
    up_weight,
    down_weight,
    kv_pool,
    block_home,
    chosen,
    chosen_count,
):
    pool_dev = kv_pool.shape[1]
    head_size = kv_pool.shape[5]
    requests, features = hidden.shape
    position = float(block_home.shape[1] * kv_pool.shape[4] - 1)
    vmem = pl.BlockSpec(memory_space=pltpu.VMEM)
    scalars = pl.BlockSpec(memory_space=pltpu.SMEM)
    anywhere = pl.BlockSpec(memory_space=pl.ANY)
    f32, bf16 = jnp.float32, jnp.bfloat16
    return pl.pallas_call(
        functools.partial(decoder_kernel, n, nt),
        out_shape=jax.ShapeDtypeStruct(hidden.shape, hidden.dtype),
        in_specs=[vmem] * 4 + [scalars] * 3 + [anywhere] * 6,
        out_specs=vmem,
        scratch_shapes=[
            pltpu.VMEM((requests, features), f32),
            pltpu.VMEM(q_weight.shape, bf16),
            pltpu.VMEM(o_weight.shape, bf16),
            pltpu.VMEM(gate_weight.shape, bf16),
            pltpu.VMEM(up_weight.shape, bf16),
            pltpu.VMEM(down_weight.shape, bf16),
            pltpu.VMEM(kv_pool.shape[:2] + kv_pool.shape[3:], bf16),
            pltpu.VMEM((LAYERS, n, LANES), f32),
            pltpu.VMEM((n, LAYERS, n, LANES), f32),
            pltpu.VMEM((LAYERS, n, PARTS, 16, q_weight.shape[2] // PARTS // 2 + LANES), bf16),
            pltpu.VMEM((8 * n, pool_dev * LANES), f32),
            pltpu.VMEM((LAYERS, n, 8 * n + 16, LANES), bf16),
            pltpu.VMEM((n, 8, 2 * WIDE + LANES), f32),
            pltpu.VMEM((LAYERS, n, 8, 2 * WIDE + LANES), f32),
            pltpu.VMEM((LAYERS, n, 16, WIDE // 2), bf16),
            pltpu.VMEM((LAYERS, 2, nt, PARTS, 16, features // PARTS // 2), bf16),
            pltpu.SemaphoreType.DMA((LAYERS, 6)),
            pltpu.SemaphoreType.DMA((n,)),
            pltpu.SemaphoreType.DMA((PHASES * LAYERS + 1, n)),
            pltpu.SemaphoreType.DMA((n,)),
            pltpu.SemaphoreType.DMA((PARTS, n)),
            pltpu.SemaphoreType.DMA((PARTS, nt)),
            pltpu.SemaphoreType.DMA((2 * LAYERS, PARTS, nt)),
        ],
        compiler_params=pltpu.CompilerParams(
            collective_id=0, has_side_effects=True, vmem_limit_bytes=62 * MIB
        ),
        name="decoder_layers",
    )(
        hidden,
        attn_gain,
        ffn_gain,
        rotary_table(head_size, position),
        block_home,
        chosen,
        jnp.transpose(chosen_count, (1, 2, 0)),
        q_weight,
        o_weight,
        gate_weight,
        up_weight,
        down_weight,
        kv_pool,
    )


def solution(mesh):
    n, nt = mesh.shape["req"], mesh.shape["tp"]
    body = functools.partial(fused_shards, n, nt) if n == 8 else shards
    return jax.shard_map(
        body,
        mesh=mesh,
        in_specs=(
            P(None, "req"),
            P(None, "req"),
            P(None, "req", "tp"),
            P(None, "tp", "req"),
            P(None, "req"),
            P(None, "req", "tp"),
            P(None, "req", "tp"),
            P(None, "tp", "req"),
            P(None, "req", "tp", None, None, None),
            P("req", None),
            P(None, "req", "tp", None),
            P(None, "req", "tp"),
        ),
        out_specs=P(None, "req"),
        check_vma=False,
    )
```

```python
import functools
import math

import jax
import jax.numpy as jnp
import numpy as np
from jax import lax
from jax.experimental import pallas as pl
from jax.experimental.pallas import tpu as pltpu
from jax.sharding import PartitionSpec as P

D = 8192
LAYERS = 2


MASK_FILL = -1e30
EPSILON = 1e-05
MESH = pl.DeviceIdType.MESH
LANES = 128
TOKENS = 512
WIDE = 512
CHIP_UNITS = 896
PARTS = 2
PHASES = 5
MIB = 1 << 20


def rotary(queries, position):
    head_size = queries.shape[-1]
    half_size = head_size // 2
    freq_idx = jnp.arange(half_size).astype(queries.dtype)
    angles = position * jnp.exp(freq_idx * (-2.0 * math.log(500000.0) / head_size))
    cosine = jnp.cos(angles)
    sine_part = jnp.sin(angles)
    lower_half = queries[..., :half_size]
    upper_half = queries[..., half_size:]
    return jnp.concatenate(
        [
            lower_half * cosine - upper_half * sine_part,
            upper_half * cosine + lower_half * sine_part,
        ],
        axis=-1,
    )


def local_squares(current):
    widened = current.astype(jnp.float32)
    return jnp.sum(widened * widened, axis=1)


def apply_gain(current, gain):
    return (current.astype(jnp.float32) * gain.astype(jnp.float32)).astype(jnp.bfloat16)


def inverse_of(squares):
    return lax.rsqrt(squares / D + EPSILON)


def summed_inverse(current):
    return inverse_of(lax.psum(local_squares(current), "req"))


def sum_over_heads(partial_sum):
    return lax.psum(partial_sum, "tp")


def block_stats(queries, blocks, valid):
    scores = jnp.einsum(
        "sigeh,sigqbh->sigeqb", queries, blocks[:, :, :, :, 0], preferred_element_type=jnp.float32
    )
    block_max = jnp.max(scores, axis=5)
    exp_terms = jnp.exp(scores - block_max[..., None])
    block_sum = jnp.sum(exp_terms, axis=5)
    block_acc = jnp.einsum(
        "sigeqb,sigqbh->sigeqh",
        exp_terms.astype(jnp.bfloat16),
        blocks[:, :, :, :, 1],
        preferred_element_type=jnp.float32,
    )
    block_max = jnp.where(valid[:, :, :, None, :], block_max, MASK_FILL)
    return (block_max, block_sum, block_acc)


def combine(block_max, block_sum, block_acc, axes):
    overall = jnp.max(block_max, axis=axes, keepdims=True)
    rescale = jnp.exp(block_max - overall)
    numerator = jnp.sum(rescale[..., None] * block_acc, axis=axes)
    denominator = jnp.sum(rescale * block_sum, axis=axes)
    return (jnp.squeeze(overall, axes), denominator, numerator)


def shards(
    hidden,
    attn_gain,
    q_weight,
    o_weight,
    ffn_gain,
    gate_weight,
    up_weight,
    down_weight,
    kv_pool,
    block_home,
    chosen,
    chosen_count,
):
    n_req = lax.axis_size("req")
    req_dev = chosen.shape[1]
    heads_dev = chosen.shape[2]
    most_sel = chosen.shape[3]
    pool_dev = kv_pool.shape[1]
    head_size = kv_pool.shape[5]
    per_store = block_home.shape[1] // n_req
    position = float(block_home.shape[1] * kv_pool.shape[4] - 1)
    own_start = lax.axis_index("req") * req_dev
    row_index = jnp.arange(req_dev)[:, None, None]
    entries = jnp.arange(most_sel)
    store_ids = jnp.arange(n_req)[:, None, None, None, None]
    slot_ids = jnp.arange(per_store)[None, None, None, :, None]
    head_index = jnp.arange(heads_dev)[None, None, :, None]
    current = hidden
    for layer_no in range(LAYERS):
        scaled = apply_gain(current, attn_gain[layer_no])
        inv_all = summed_inverse(current)
        rows_in = scaled
        product = jnp.dot(rows_in, q_weight[layer_no], preferred_element_type=jnp.float32)
        summed = lax.psum_scatter(product, "req", scatter_dimension=0, tiled=True)
        inv_own = lax.dynamic_slice_in_dim(inv_all, own_start, req_dev, 0)
        queries = (summed * inv_own[:, None]).reshape(req_dev, heads_dev, -1, head_size)
        queries = (rotary(queries, position) * head_size ** (-0.5)).astype(jnp.bfloat16)
        pool_ids = block_home[row_index, chosen[layer_no]]
        home_store = pool_ids // pool_dev
        home_slot = pool_ids % pool_dev
        used_mask = entries[None, None, :] < chosen_count[layer_no][:, :, None]
        earlier = (
            (home_store[..., :, None] == home_store[..., None, :])
            & used_mask[..., None, :]
            & (entries[None, :] < entries[:, None])
        )
        rank = jnp.sum(earlier.astype(jnp.int32), axis=-1)
        match = (
            (home_store[None, :, :, None, :] == store_ids)
            & (rank[None, :, :, None, :] == slot_ids)
            & used_mask[None, :, :, None, :]
        )
        wanted = jnp.sum(jnp.where(match, home_slot[None, :, :, None, :] + 1, 0), axis=4) - 1
        received_ids = lax.all_to_all(wanted, "req", split_axis=0, concat_axis=0, tiled=True)
        served = kv_pool[layer_no][jnp.maximum(received_ids, 0), head_index]
        fetched = lax.all_to_all(served, "req", split_axis=0, concat_axis=0, tiled=True)
        spread = jnp.broadcast_to(queries[None], (n_req,) + queries.shape)
        stats = block_stats(spread, fetched, wanted >= 0)
        overall, denominator, numerator = combine(stats[0], stats[1], stats[2], (0, 4))
        context = (numerator / denominator[..., None]).astype(jnp.bfloat16).reshape(req_dev, -1)
        attn_part = jnp.dot(
            lax.all_gather(context, "req", axis=0, tiled=True),
            o_weight[layer_no],
            preferred_element_type=jnp.float32,
        )
        attended = (current.astype(jnp.float32) + sum_over_heads(attn_part)).astype(jnp.bfloat16)
        scaled = apply_gain(attended, ffn_gain[layer_no])
        inv_all = summed_inverse(attended)
        gate = jnp.dot(scaled, gate_weight[layer_no], preferred_element_type=jnp.float32)
        up_part = jnp.dot(scaled, up_weight[layer_no], preferred_element_type=jnp.float32)
        payload = (gate, up_part)
        totals = lax.psum((payload[0], payload[1]), "req")
        gate = totals[0] * inv_all[:, None]
        up_part = totals[1] * inv_all[:, None]
        activated = (jax.nn.silu(gate) * up_part).astype(jnp.bfloat16)
        ffn_part = jnp.dot(activated, down_weight[layer_no], preferred_element_type=jnp.float32)
        current = (attended.astype(jnp.float32) + sum_over_heads(ffn_part)).astype(jnp.bfloat16)
    return current


def decoder_kernel(
    n,
    nt,
    hidden_ref,
    attn_gain_ref,
    ffn_gain_ref,
    turn_ref,
    home_ref,
    chosen_ref,
    count_ref,
    q_hbm,
    o_hbm,
    gate_hbm,
    up_hbm,
    down_hbm,
    kv_hbm,
    out_ref,
    state,
    q_w,
    o_w,
    gate_w,
    up_w,
    down_w,
    kv_w,
    used_out,
    used_all,
    q_in,
    scores,
    part_in,
    ffn_out,
    ffn_in,
    act_all,
    head_sums,
    load_sem,
    send_sem,
    recv_sem,
    used_sem,
    q_send_sem,
    tp_send_sem,
    tp_recv_sem,
):
    me = lax.axis_index("req")
    my_tp = lax.axis_index("tp")
    hd = LANES
    order = range(1, n)
    slots = kv_w.shape[1]

    def load(layer, which):
        source, target = (
            (q_hbm, q_w),
            (kv_hbm, kv_w),
            (o_hbm, o_w),
            (gate_hbm, gate_w),
            (up_hbm, up_w),
            (down_hbm, down_w),
        )[which]
        if which == 1:
            source = source.at[layer, :, 0]
        else:
            source = source.at[layer]
        return pltpu.make_async_copy(source, target.at[layer], load_sem.at[layer, which])

    def peer(step):
        kind = (step - 1) // 2
        row = (me // 4 + 1 - kind // 2) % 2
        column = (me // 2 + 1 - kind % 2) % 2
        return row * 4 + column * 2 + (me + step) % 2

    def send(source, target, step, phase):
        return pltpu.make_async_remote_copy(
            src_ref=source,
            dst_ref=target,
            send_sem=send_sem.at[step],
            recv_sem=recv_sem.at[phase, me],
            device_id=(peer(step), my_tp),
            device_id_type=MESH,
        )

    def wait_from(slot, who, phase):
        pltpu.make_async_remote_copy(
            src_ref=slot,
            dst_ref=slot,
            send_sem=send_sem.at[0],
            recv_sem=recv_sem.at[phase, who],
            device_id=(who, my_tp),
            device_id_type=MESH,
        ).wait_recv()

    def exchange(source_of, target, phase):
        copies = [send(source_of(peer(step)), target.at[me], step, phase) for step in order]
        for copy in copies:
            copy.start()
        return copies

    def finish(copies, target, phase):
        for copy in copies:
            copy.wait_send()
        for step in range(n - 1, 0, -1):
            who = peer(step)
            wait_from(target.at[who], who, phase)

    def head_copy(slot, step, phase, part, who):
        return pltpu.make_async_remote_copy(
            src_ref=slot,
            dst_ref=slot,
            send_sem=tp_send_sem.at[part, step],
            recv_sem=tp_recv_sem.at[phase, part, who],
            device_id=(me, lax.rem(my_tp + step, nt)),
            device_id_type=MESH,
        )

    def over_heads(product_of, buffer, phase):
        copies = []
        for part in range(PARTS):
            product = product_of(part)
            width = product.shape[1] // 2
            packed = jnp.concatenate([product[:, :width], product[:, width:]], axis=0)
            buffer[my_tp, part] = packed.astype(jnp.bfloat16)
            for step in range(1, nt):
                copy = head_copy(buffer.at[my_tp, part], step, phase, part, my_tp)
                copy.start()
                copies.append(copy)
        for copy in copies:
            copy.wait_send()
        for part in range(PARTS):
            for step in range(1, nt):
                who = lax.rem(my_tp + step, nt)
                head_copy(buffer.at[who, part], step, phase, part, who).wait_recv()
            total = buffer[0, part].astype(jnp.float32)
            for index in range(1, nt):
                total = total + buffer[index, part].astype(jnp.float32)
            total = jnp.concatenate([total[0:8], total[8:16]], axis=1)
            width = total.shape[1]
            columns = slice(part * width, (part + 1) * width)
            state[:, columns] = (state[:, columns] + total).astype(jnp.bfloat16).astype(jnp.float32)

    def normed(gain_ref, layer):
        current = state[...]
        gains = gain_ref[...].astype(jnp.float32)
        gain = jnp.where(layer == 0, gains[0:1], gains[1:2])
        squares = jnp.sum(current * current, axis=1, keepdims=True)
        return (current * gain).astype(jnp.bfloat16), jnp.broadcast_to(squares, (current.shape[0], LANES))

    def chip_units(chip):
        return pl.ds(pl.multiple_of(chip * CHIP_UNITS, LANES), CHIP_UNITS)

    for which in range(3):
        load(0, which).start()

    barrier = pltpu.get_barrier_semaphore()
    for step in range(1, n):
        pl.semaphore_signal(barrier, inc=1, device_id=(peer(step), my_tp), device_id_type=MESH)
    for step in range(1, nt):
        pl.semaphore_signal(
            barrier, inc=1, device_id=(me, lax.rem(my_tp + step, nt)), device_id_type=MESH
        )
    state[...] = hidden_ref[...].astype(jnp.float32)

    def query_slot(layer, who, part):
        width = q_in.shape[4] - (LANES if part else 0)
        return q_in.at[layer, who, part, :, 0:width]

    def query_copies(layer, part):
        return [
            pltpu.make_async_remote_copy(
                src_ref=query_slot(layer, me, part),
                dst_ref=query_slot(layer, me, part),
                send_sem=q_send_sem.at[part, step],
                recv_sem=recv_sem.at[PHASES * layer + part, me],
                device_id=(peer(step), my_tp),
                device_id_type=MESH,
            )
            for step in order
        ]

    def query_product(layer, sending):
        scaled, squares = normed(attn_gain_ref, layer)
        load(layer, 0).wait()
        high = squares.astype(jnp.bfloat16).astype(jnp.float32)
        tail = jnp.concatenate([high, squares - high], axis=0)
        width = q_w.shape[2] // PARTS
        for part in range(PARTS):
            product = jnp.dot(
                scaled,
                q_w[layer, :, part * width : (part + 1) * width],
                preferred_element_type=jnp.float32,
            )
            packed = jnp.concatenate([product[:, : width // 2], product[:, width // 2 :]], axis=0)
            q_in[layer, me, part] = jnp.concatenate([packed, tail], axis=1).astype(jnp.bfloat16)
            if sending:
                for copy in query_copies(layer, part):
                    copy.start()

    query_product(0, False)
    for which in (3, 4):
        load(0, which).start()
    pl.semaphore_wait(barrier, n - 1 + nt - 1)

    def used_copy(step):
        return pltpu.make_async_remote_copy(
            src_ref=used_out,
            dst_ref=used_all.at[me],
            send_sem=used_sem.at[step],
            recv_sem=recv_sem.at[PHASES * LAYERS, me],
            device_id=(peer(step), my_tp),
            device_id_type=MESH,
        )

    for part in range(PARTS):
        for copy in query_copies(0, part):
            copy.start()
    rows8 = lax.broadcasted_iota(jnp.int32, (n, LANES), 0)
    lanes8 = lax.broadcasted_iota(jnp.int32, (n, LANES), 1)
    slot_ids = jnp.where(lanes8 < slots, rows8 * slots + lanes8, -1)
    for layer in range(LAYERS):
        used = jnp.zeros((n, LANES), jnp.float32)
        for entry in range(chosen_ref.shape[3]):
            slot = home_ref[0, chosen_ref[layer, 0, 0, entry]]
            slot = jnp.where(entry < count_ref[0, 0, layer], slot, -2)
            used = jnp.where(slot_ids == slot, 1.0, used)
        used_out[layer] = used
    for step in order:
        used_copy(step).start()
    used_all[me] = used_out[...]

    def layer_body(layer, carry):
        phase = PHASES * layer
        load(layer, 1).wait()

        @pl.when(layer == 0)
        def _():
            for step in range(1, n):
                wait_from(used_all.at[peer(step)], peer(step), PHASES * LAYERS)
                used_copy(step).wait_send()

        used = jnp.zeros((8, LANES), jnp.float32)
        for who in range(n):
            row = jnp.where(rows8 == me, used_all[who, layer], 0.0)
            used = jnp.where(rows8 == who, jnp.sum(row, axis=0, keepdims=True), used)
        for part in range(PARTS):
            for copy in query_copies(layer, part):
                copy.wait_send()
        heads = []
        for part in range(PARTS):
            for step in range(n - 1, 0, -1):
                who = peer(step)
                wait_from(query_slot(layer, who, part), who, phase + part)
            total = query_slot(layer, 0, part)[...].astype(jnp.float32)
            for who in range(1, n):
                total = total + query_slot(layer, who, part)[...].astype(jnp.float32)
            width = q_in.shape[4] - LANES
            if part == 0:
                squares = total[0:8, width:] + total[8:16, width:]
                inv = lax.rsqrt(squares / D + EPSILON)
            for half in range(2):
                for head in range(width // hd):
                    heads.append(total[half * 8 : half * 8 + 8, head * hd : (head + 1) * hd] * inv)
        queries = []
        for query in heads:
            swapped = jnp.concatenate([query[:, hd // 2 :], query[:, : hd // 2]], axis=1)
            queries.append((query * turn_ref[0:8] + swapped * turn_ref[8:16]) * hd ** (-0.5))
        queries = jnp.concatenate(queries, axis=0).astype(jnp.bfloat16)

        load(layer, 5).start()
        step_slots = TOKENS // LANES
        peak = jnp.full((n * 8, LANES), MASK_FILL, jnp.float32)
        for chunk in range(slots // step_slots):
            keys = kv_w[layer, chunk * step_slots : (chunk + 1) * step_slots, 0].reshape(TOKENS, hd)
            block = lax.dot_general(
                queries, keys, (((1,), (1,)), ((), ())), preferred_element_type=jnp.float32
            )
            for k in range(step_slots):
                slot = chunk * step_slots + k
                mask = jnp.broadcast_to(used[:, slot : slot + 1], (8, LANES)) > 0.5
                mask = jnp.broadcast_to(mask[None], (n, 8, LANES))
                piece = block[:, k * LANES : (k + 1) * LANES].reshape(n, 8, LANES)
                piece = jnp.where(mask, piece, MASK_FILL).reshape(n * 8, LANES)
                scores[:, slot * LANES : (slot + 1) * LANES] = piece
                peak = jnp.maximum(peak, piece)
        top = jnp.max(peak, axis=1, keepdims=True)
        sums = jnp.zeros((n * 8, LANES), jnp.float32)
        acc = jnp.zeros((n * 8, hd), jnp.float32)
        for chunk in range(slots // step_slots):
            terms = jnp.exp(scores[:, chunk * TOKENS : (chunk + 1) * TOKENS] - top)
            for k in range(step_slots):
                sums = sums + terms[:, k * LANES : (k + 1) * LANES]
            values = kv_w[layer, chunk * step_slots : (chunk + 1) * step_slots, 1].reshape(TOKENS, hd)
            acc = acc + jnp.dot(terms.astype(jnp.bfloat16), values, preferred_element_type=jnp.float32)
        total = jnp.sum(sums, axis=1, keepdims=True)
        level = top + jnp.log(total)
        stats = jnp.zeros((8, LANES), jnp.float32)
        lane = lax.broadcasted_iota(jnp.int32, (8, LANES), 1)
        for head in range(n):
            stats = jnp.where(lane == head, level[head * 8 : (head + 1) * 8], stats)
        high = stats.astype(jnp.bfloat16).astype(jnp.float32)
        payload = jnp.concatenate([acc / total, high, stats - high], axis=0)
        part_in[layer, me] = payload.astype(jnp.bfloat16)
        copies = exchange(lambda who: part_in.at[layer, me], part_in.at[layer], phase + 2)
        load(layer, 2).wait()
        finish(copies, part_in.at[layer], phase + 2)

        rows = 8 * n
        levels = []
        for who in range(n):
            pair = part_in[layer, who, rows : rows + 16].astype(jnp.float32)
            levels.append(pair[0:8] + pair[8:16])
        overall = functools.reduce(jnp.maximum, levels)
        shares = [jnp.exp(level - overall) for level in levels]
        denominator = functools.reduce(jnp.add, shares)
        context = [jnp.zeros((8, hd), jnp.float32) for _ in range(n)]
        for who in range(n):
            share = shares[who] / denominator
            parts = part_in[layer, who, 0:rows].astype(jnp.float32)
            for head in range(n):
                context[head] = context[head] + share[:, head : head + 1] * parts[head * 8 : (head + 1) * 8]
        context = jnp.concatenate(context, axis=1).astype(jnp.bfloat16)

        width = state.shape[1] // PARTS

        @pl.when(layer + 1 < LAYERS)
        def _():
            for which in (0, 1, 2):
                load(layer + 1, which).start()

        def out_part(part):
            weight = o_w[layer, :, part * width : (part + 1) * width]
            return jnp.dot(context, weight, preferred_element_type=jnp.float32)

        over_heads(out_part, head_sums.at[layer, 0], 2 * layer)

        scaled, squares = normed(ffn_gain_ref, layer)
        load(layer, 3).wait()
        load(layer, 4).wait()

        def gate_up(chip):
            for index, weight in enumerate((gate_w, up_w)):
                product = jnp.dot(scaled, weight[layer, :, chip_units(chip)], preferred_element_type=jnp.float32)
                columns = slice(index * WIDE, (index + 1) * WIDE)
                ffn_out[2 * chip, :, columns] = product[:, 0:WIDE]
                ffn_out[2 * chip + 1, :, columns] = product[:, CHIP_UNITS - WIDE :]
            ffn_out[2 * chip, :, 2 * WIDE :] = squares
            ffn_out[2 * chip + 1, :, 2 * WIDE :] = squares

        def ffn_send(step):
            return send(ffn_out.at[peer(step)], ffn_in.at[layer, me], step, phase + 3)

        def ffn_step(kind, carry):
            gate_up(peer(2 * kind + 1) // 2)
            ffn_send(2 * kind + 1).start()
            ffn_send(2 * kind + 2).start()
            return carry

        lax.fori_loop(0, n // 2 - 1, ffn_step, 0)

        @pl.when(layer + 1 < LAYERS)
        def _():
            load(layer + 1, 3).start()

        gate_up(me // 2)
        ffn_send(n - 1).start()
        ffn_in[layer, me] = ffn_out[me]
        copies = [ffn_send(step) for step in order]
        finish(copies, ffn_in.at[layer], phase + 3)
        total = ffn_in[layer, 0]
        for who in range(1, n):
            total = total + ffn_in[layer, who]
        inv = lax.rsqrt(total[:, 2 * WIDE :] / D + EPSILON)[:, 0:1]
        gate = total[:, 0:WIDE] * inv
        up = total[:, WIDE : 2 * WIDE] * inv
        act = gate / (1.0 + jnp.exp(-gate)) * up
        packed = jnp.concatenate([act[:, 0 : WIDE // 2], act[:, WIDE // 2 :]], axis=0)
        act_all[layer, me] = packed.astype(jnp.bfloat16)
        copies = exchange(lambda who: act_all.at[layer, me], act_all.at[layer], phase + 4)
        load(layer, 5).wait()

        def chip_act(chip):
            shares = []
            for core in range(2):
                packed = act_all[layer, 2 * chip + core].astype(jnp.float32)
                shares.append(jnp.concatenate([packed[0:8], packed[8:16]], axis=1))
            both = [shares[0], shares[1][:, 2 * WIDE - CHIP_UNITS :]]
            return jnp.concatenate(both, axis=1).astype(jnp.bfloat16)

        def arrived(step):
            wait_from(act_all.at[layer, peer(step)], peer(step), phase + 4)

        arrived(n - 1)
        sums = jnp.dot(
            chip_act(me // 2), down_w[layer, chip_units(me // 2), :], preferred_element_type=jnp.float32
        )
        for copy in copies:
            copy.wait_send()
        for kind in range(n // 2 - 2, 0, -1):
            arrived(2 * kind + 1)
            arrived(2 * kind + 2)
            chip = peer(2 * kind + 1) // 2
            sums = sums + jnp.dot(
                chip_act(chip), down_w[layer, chip_units(chip), :], preferred_element_type=jnp.float32
            )
        arrived(1)
        arrived(2)
        last = peer(1) // 2
        act = chip_act(last)

        @pl.when(layer + 1 < LAYERS)
        def _():
            load(layer + 1, 4).start()

        def down_part(part):
            columns = slice(part * width, (part + 1) * width)
            weight = down_w[layer, chip_units(last), columns]
            return sums[:, columns] + jnp.dot(act, weight, preferred_element_type=jnp.float32)

        over_heads(down_part, head_sums.at[layer, 1], 2 * layer + 1)

        @pl.when(layer + 1 < LAYERS)
        def _():
            query_product(layer + 1, True)

        return carry

    lax.fori_loop(0, LAYERS, layer_body, 0)
    out_ref[...] = state[...].astype(out_ref.dtype)


def rotary_table(head_size, position):
    freq = np.arange(head_size // 2, dtype=np.float64)
    angles = position * np.exp(freq * (-2.0 * math.log(500000.0) / head_size))
    cosine = np.concatenate([np.cos(angles), np.cos(angles)])
    sine = np.concatenate([-np.sin(angles), np.sin(angles)])
    table = np.concatenate([np.tile(cosine[None], (8, 1)), np.tile(sine[None], (8, 1))])
    return jnp.asarray(table, jnp.float32)


def fused_shards(
    n,
    nt,
    hidden,
    attn_gain,
    q_weight,
    o_weight,
    ffn_gain,
    gate_weight,
    up_weight,
    down_weight,
    kv_pool,
    block_home,
    chosen,
    chosen_count,
):
    pool_dev = kv_pool.shape[1]
    head_size = kv_pool.shape[5]
    requests, features = hidden.shape
    position = float(block_home.shape[1] * kv_pool.shape[4] - 1)
    vmem = pl.BlockSpec(memory_space=pltpu.VMEM)
    scalars = pl.BlockSpec(memory_space=pltpu.SMEM)
    anywhere = pl.BlockSpec(memory_space=pl.ANY)
    f32, bf16 = jnp.float32, jnp.bfloat16
    return pl.pallas_call(
        functools.partial(decoder_kernel, n, nt),
        out_shape=jax.ShapeDtypeStruct(hidden.shape, hidden.dtype),
        in_specs=[vmem] * 4 + [scalars] * 3 + [anywhere] * 6,
        out_specs=vmem,
        scratch_shapes=[
            pltpu.VMEM((requests, features), f32),
            pltpu.VMEM(q_weight.shape, bf16),
            pltpu.VMEM(o_weight.shape, bf16),
            pltpu.VMEM(gate_weight.shape, bf16),
            pltpu.VMEM(up_weight.shape, bf16),
            pltpu.VMEM(down_weight.shape, bf16),
            pltpu.VMEM(kv_pool.shape[:2] + kv_pool.shape[3:], bf16),
            pltpu.VMEM((LAYERS, n, LANES), f32),
            pltpu.VMEM((n, LAYERS, n, LANES), f32),
            pltpu.VMEM((LAYERS, n, PARTS, 16, q_weight.shape[2] // PARTS // 2 + LANES), bf16),
            pltpu.VMEM((8 * n, pool_dev * LANES), f32),
            pltpu.VMEM((LAYERS, n, 8 * n + 16, LANES), bf16),
            pltpu.VMEM((n, 8, 2 * WIDE + LANES), f32),
            pltpu.VMEM((LAYERS, n, 8, 2 * WIDE + LANES), f32),
            pltpu.VMEM((LAYERS, n, 16, WIDE // 2), bf16),
            pltpu.VMEM((LAYERS, 2, nt, PARTS, 16, features // PARTS // 2), bf16),
            pltpu.SemaphoreType.DMA((LAYERS, 6)),
            pltpu.SemaphoreType.DMA((n,)),
            pltpu.SemaphoreType.DMA((PHASES * LAYERS + 1, n)),
            pltpu.SemaphoreType.DMA((n,)),
            pltpu.SemaphoreType.DMA((PARTS, n)),
            pltpu.SemaphoreType.DMA((PARTS, nt)),
            pltpu.SemaphoreType.DMA((2 * LAYERS, PARTS, nt)),
        ],
        compiler_params=pltpu.CompilerParams(
            collective_id=0, has_side_effects=True, vmem_limit_bytes=62 * MIB
        ),
        name="decoder_layers",
    )(
        hidden,
        attn_gain,
        ffn_gain,
        rotary_table(head_size, position),
        block_home,
        chosen,
        jnp.transpose(chosen_count, (1, 2, 0)),
        q_weight,
        o_weight,
        gate_weight,
        up_weight,
        down_weight,
        kv_pool,
    )


def solution(mesh):
    n, nt = mesh.shape["req"], mesh.shape["tp"]
    body = functools.partial(fused_shards, n, nt) if n == 8 else shards
    return jax.shard_map(
        body,
        mesh=mesh,
        in_specs=(
            P(None, "req"),
            P(None, "req"),
            P(None, "req", "tp"),
            P(None, "tp", "req"),
            P(None, "req"),
            P(None, "req", "tp"),
            P(None, "req", "tp"),
            P(None, "tp", "req"),
            P(None, "req", "tp", None, None, None),
            P("req", None),
            P(None, "req", "tp", None),
            P(None, "req", "tp"),
        ),
        out_specs=P(None, "req"),
        check_vma=False,
    )
```
